512 devices in a mesh: tm: 16 (over y, x), space: 32 (over z, core).
Axes of the slice: x: 4, y: 4, z: 16, core: 2. Of those that a mesh axis runs over, the one named last changes fastest.
Arguments:
- source: float32 [32, 8192, 128], P('tm', 'space'), may hold values from -6 to 6
- elem_scale: float32 [8192], P('space'), may hold values from 1 to 2
- diag_block: float32 [128, 128], replicated, as said below
- block_inverse: float32 [128, 128], replicated, as said below
- face_flux: float32 [4, 128, 128], replicated, may hold values from -0.072 to 0.072
- time_trace: float32 [128, 128], replicated, as said below
- neighbours: int32 [8192, 4], P('space'), may hold values from 0 to 287, as said below
- send_rows: int32 [32, 32], P('space'), may hold values from 0 to 255, as said below
Outputs:
- smoothed: float32 [32, 8192, 128], P('tm', 'space')
The draws below stay inside these ranges and needn't reach their ends.
Inputs may be any that keep to these rules, and one draw needn't show every extreme that they name: `neighbours`: indexes the extended list of the element's own partition, of 288 positions; each of the 32 received positions is named by exactly one face of the partition's elements, and only the partition's sent elements name received positions. `send_rows`: each row holds 32 distinct local positions of its partition's elements. `diag_block`: the identity plus a skew-symmetric matrix plus a positive semidefinite matrix. `block_inverse`: the inverse of diag_block. `time_trace`: its largest singular value is at most 0.9.
All inputs are finite; a program needn't handle non-finite values.
Results may differ from the reference program's by a relative error of at most 0.0001.
Values sent between devices are 32-bit elements; how exact they have to be, the bound alone decides.
A program may use at most 64 MiB of HBM per device.

```python
import math
import jax
import jax.numpy as jnp
from jax import lax

U = 128
E_DEV = 256
HB = 16
NT = 32
NE = 8192


def skew_part(key, number):
    first = jax.random.normal(jax.random.fold_in(key, number), (U, U), jnp.float32) * (0.3 / math.sqrt(U))
    return (first - first.T) / math.sqrt(2.0)


def block_pair(key):
    skew = skew_part(key, 11)
    second = jax.random.normal(jax.random.fold_in(key, 12), (U, U), jnp.float32)
    diffusion = jnp.dot(second, second.T) * (0.1 / U)
    block = jnp.eye(U, dtype=jnp.float32) + skew + diffusion
    return (block, jnp.linalg.inv(block))


def draw_diag_block(key, part):
    return block_pair(key)[0]


def draw_block_inverse(key, part):
    return block_pair(key)[1]


def draw_time_trace(key, part):
    skew = skew_part(key, 21)
    return 0.9 * jnp.linalg.inv(jnp.eye(U, dtype=jnp.float32) + skew)


def shuffle_one(subkey):
    return jax.random.permutation(subkey, E_DEV).astype(jnp.int32)


def place_value(order, value, slot):
    held = order[slot]
    order = jnp.where(order == value, held, order)
    return order.at[slot].set(value)


def fix_order(order):
    order = place_value(order, E_DEV - 1, 0)
    return place_value(order, 0, HB)


def rank_of(order):
    return jnp.zeros((E_DEV,), jnp.int32).at[order].set(jnp.arange(E_DEV, dtype=jnp.int32))


def boundary_layout(key):
    partitions = NE // E_DEV
    key_list = jax.random.split(jax.random.fold_in(key, 31), partitions)
    orders = jax.vmap(shuffle_one)(key_list)
    chosen = jax.random.randint(jax.random.fold_in(key, 32), (), 0, partitions)
    fixed = jax.vmap(fix_order)(orders)
    pick = jnp.arange(partitions, dtype=jnp.int32)[:, None] == chosen
    orders = jnp.where(pick, fixed, orders).astype(jnp.int32)
    ranks = jax.vmap(rank_of)(orders)
    return (orders, ranks)


def draw_send_rows(key, part):
    orders, ranks = boundary_layout(key)
    return orders[:, :2 * HB].astype(jnp.int32)


def draw_neighbours(key, part):
    partitions = NE // E_DEV
    orders, ranks = boundary_layout(key)
    columns = []
    for face_index in range(4):
        key_list = jax.random.split(jax.random.fold_in(key, 40 + face_index), partitions)
        columns.append(jax.vmap(shuffle_one)(key_list))
    received = (E_DEV + ranks).astype(jnp.int32)
    columns[2] = jnp.where(ranks < HB, received, columns[2])
    columns[3] = jnp.where((ranks >= HB) & (ranks < 2 * HB), received, columns[3])
    stacked = jnp.stack(columns, axis=-1)
    return stacked.reshape(NE, 4).astype(jnp.int32)


def levels(stream_key, extent, cuts, least, top_value):
    gain = 1.0
    for dim, blocks in cuts:
        steps = jax.random.uniform(jax.random.fold_in(jax.random.fold_in(stream_key, 6), dim), (blocks,), jnp.float32, least / len(cuts), top_value / len(cuts))
        gain = gain * jnp.repeat(jnp.exp(steps), extent[dim] // blocks).reshape((-1,) + (1,) * (len(extent) - 1 - dim))
    return gain


def normal_values(key, dims, scale, most, pieces=(), held_as=jnp.bfloat16):
    array = jax.random.normal(key, dims, jnp.float32) * scale
    if len(pieces) > 0:
        array = levels(key, dims, pieces, -0.22, 0.18) * array
    return jnp.clip(array, min=-most, max=most).astype(held_as)


def setup_inputs(seed: int = 0) -> dict:
    arg_keys = jax.random.split(jax.random.key(seed), 9)
    source = normal_values(arg_keys[0], (NT, NE, U), 1.0, 6.0, ((0, 16), (1, 32)), jnp.float32)
    elem_scale = jnp.clip(jnp.exp(math.log(2.0) - 0.6931472 * jax.random.uniform(arg_keys[1], (NE,), jnp.float32) ** levels(arg_keys[1], (NE,), ((0, 32),), -0.2, 0.2)), 1.0, 2.0)
    diag_block = draw_diag_block(jax.random.fold_in(arg_keys[8], 71), 0)
    block_inverse = draw_block_inverse(jax.random.fold_in(arg_keys[8], 71), 0)
    face_flux = normal_values(arg_keys[4], (4, U, U), 0.012, 0.072, (), jnp.float32)
    time_trace = draw_time_trace(jax.random.fold_in(arg_keys[8], 71), 0)
    neighbours = draw_neighbours(jax.random.fold_in(arg_keys[8], 71), 0)
    send_rows = draw_send_rows(jax.random.fold_in(arg_keys[8], 71), 0)
    return {"source": source, "elem_scale": elem_scale, "diag_block": diag_block, "block_inverse": block_inverse, "face_flux": face_flux, "time_trace": time_trace, "neighbours": neighbours, "send_rows": send_rows}


DAMPING = 0.7

def product(left, right):
    return jnp.dot(left.astype(jnp.float32), right.astype(jnp.float32), precision=lax.Precision.HIGHEST, preferred_element_type=jnp.float32)

def reference(source, elem_scale, diag_block, block_inverse, face_flux, time_trace, neighbours, send_rows):
    partitions = NE // E_DEV
    halo_rows = HB
    face_ids = neighbours.reshape(partitions, E_DEV, 4)
    inv_scale = 1.0 / elem_scale

    def apply_slab(slab_pair):
        current, before = slab_pair
        blocks = current.reshape(partitions, E_DEV, U)
        outgoing = jnp.take_along_axis(blocks, send_rows[:, :, None], axis=1)
        from_left = jnp.roll(outgoing[:, halo_rows:], 1, axis=0)
        from_right = jnp.roll(outgoing[:, :halo_rows], -1, axis=0)
        extended = jnp.concatenate([blocks, from_left, from_right], axis=1)
        face_term = jnp.zeros((NE, U), jnp.float32)
        for face_index in range(4):
            picked = jnp.take_along_axis(extended, face_ids[:, :, face_index][:, :, None], axis=1)
            face_term = face_term + product(picked.reshape(NE, U), face_flux[face_index])
        diagonal_term = product(current, diag_block) * elem_scale[:, None]
        return diagonal_term - product(before, time_trace) - face_term

    def operate(field):
        earlier = jnp.concatenate([jnp.zeros_like(field[:1]), field[:-1]], axis=0)
        return lax.map(apply_slab, (field, earlier))

    def smooth(solution):
        residual = source - operate(solution)
        return solution + DAMPING * product(residual, block_inverse) * inv_scale[None, :, None]
    solution = DAMPING * product(source, block_inverse) * inv_scale[None, :, None]
    solution = smooth(solution)
    residual = source - operate(solution)
    coarse_rhs = residual.reshape(NT // 2, 2, NE, U)
    coarse_rhs = coarse_rhs[:, 0] + coarse_rhs[:, 1]
    coarse_scale = 1.0 / (2.0 * elem_scale - 1.0)

    def coarse_step(state, rhs_slab):
        state = coarse_scale[:, None] * product(rhs_slab + product(state, time_trace), block_inverse)
        return (state, state)
    zero_state = jnp.zeros((NE, U), jnp.float32)
    final_state, correction = lax.scan(coarse_step, zero_state, coarse_rhs)
    solution = solution + jnp.repeat(correction, 2, axis=0)
    solution = smooth(solution)
    solution = smooth(solution)
    return solution
```

```python
import jax
import jax.numpy as jnp
from jax import lax
from jax.experimental import pallas as pl
from jax.experimental.pallas import tpu as pltpu
from jax.sharding import PartitionSpec as P

DAMPING = 0.7
F32 = jnp.float32
BF16 = jnp.bfloat16
MESH = pl.DeviceIdType.MESH


def dot(left, right):
    return jnp.dot(left, right, preferred_element_type=F32)


def split(x):
    high = x.astype(BF16)
    low = (x - high.astype(F32)).astype(BF16)
    return jnp.concatenate([high, low], axis=1)


def halves(x):
    width = x.shape[1] // 2
    return x[:, :width] + x[:, width:]


def weights(matrix):
    parts = split(matrix)
    return jnp.concatenate([parts, parts], axis=0)


def iota(shape, dim):
    return lax.broadcasted_iota(jnp.int32, shape, dim)


def column(row):
    size = row.shape[1]
    same = iota((size, size), 0) == iota((size, size), 1)
    return jnp.sum(jnp.where(same, row, 0.0), axis=1, keepdims=True)


def later(blocks, by):
    zeros = jnp.zeros((16 * by, blocks.shape[1]), F32)
    return jnp.concatenate([zeros, blocks[: -16 * by]], axis=0)


def kernel(
    groups, partitions,
    source_hbm, scale_hbm, inverse_hbm, flux_hbm, trace_hbm, neighbours_hbm, send_hbm,
    out_ref,
    source, scale_row, inverse, flux, trace, neighbours, send_row,
    pick, halo_pick, face_w, time_w, near_w, far_w, gathered,
    v0_last, v0_sent, v1_sent, c_sent, v3_sent, v3_last,
    halo0, halo1, halo_c, halo3, before0, before_sent, before3,
    rhs, rhs_all, chain_out, chain_all, scale_full,
    in_sem, send_sem, recv_sem,
):
    k = lax.axis_index("tm")
    p = lax.axis_index("space")
    loads = [
        pltpu.make_async_copy(src, dst, in_sem.at[i])
        for i, (src, dst) in enumerate(
            [
                (scale_hbm, scale_row), (send_hbm, send_row), (source_hbm, source), (inverse_hbm, inverse),
                (neighbours_hbm, neighbours), (flux_hbm, flux), (trace_hbm, trace),
            ]
        )
    ]
    for load in loads:
        load.start()
    left = {"space": lax.rem(p + partitions - 1, partitions)}
    right = {"space": lax.rem(p + 1, partitions)}
    others = [lax.rem(k + d, groups) for d in range(1, groups)]
    after = {"tm": others[0]}

    barrier = pltpu.get_barrier_semaphore()
    for partner in [left, right] + [{"tm": other} for other in others]:
        pl.semaphore_signal(barrier, inc=1, device_id=partner, device_id_type=MESH)

    def remote(src, dst, number, device):
        return pltpu.make_async_remote_copy(
            src_ref=src, dst_ref=dst, send_sem=send_sem.at[number], recv_sem=recv_sem.at[number],
            device_id=device, device_id_type=MESH,
        )

    def halo_copies(sent, received, number):
        if len(sent.shape) == 3:
            return [
                remote(sent.at[:, 16:32], received.at[:, 0:16], number, right),
                remote(sent.at[:, 0:16], received.at[:, 16:32], number + 1, left),
            ]
        return [
            remote(sent.at[16:32], received.at[0:16], number, right),
            remote(sent.at[0:16], received.at[16:32], number + 1, left),
        ]

    for load in loads[:4]:
        load.wait()
    scale = column(scale_row[...])
    scale_full[...] = jnp.broadcast_to(scale, (256, 128))
    sigma = DAMPING / scale
    coarse = 1.0 / (2.0 * scale - 1.0)
    send_col = column(send_row[...].astype(F32))
    choose = iota((32, 256), 1).astype(F32) == send_col
    sent_sigma = DAMPING / jnp.sum(jnp.where(choose, scale_row[...], 0.0), axis=1, keepdims=True)
    choose = jnp.where(choose, 1.0, 0.0).astype(BF16)
    inverse_w = weights(inverse[...])
    a0 = halves(dot(split(source[0]), inverse_w))
    a1 = halves(dot(split(source[1]), inverse_w))
    v0_0 = sigma * a0
    v0_1 = sigma * a1
    v0_last[...] = v0_1
    s0 = split(v0_0)
    s1 = split(v0_1)
    v0_sent[0] = halves(dot(choose, s0))
    v0_sent[1] = halves(dot(choose, s1))
    pl.semaphore_wait(barrier, groups + 1)

    first_halo = halo_copies(v0_sent, halo0, 0)
    first_sent = remote(v0_sent.at[1], before_sent, 2, after)
    first_last = remote(v0_last, before0, 3, after)
    for copy in first_halo + [first_sent, first_last]:
        copy.start()

    for load in loads[4:]:
        load.wait()
    flux_b = halves(dot(split(flux[...].reshape(512, 128)), inverse_w))
    for f in range(4):
        face_w[f * 256 : (f + 1) * 256, :] = weights(flux_b[f * 128 : (f + 1) * 128])
    m1 = halves(dot(split(trace[...]), inverse_w))
    w1 = weights(m1)
    time_w[...] = w1
    lanes = iota((256, 256), 1).astype(F32)
    lane = iota((256, 128), 1)
    halo_hit = jnp.zeros((256, 128), F32)
    for f in range(4):
        names = column(neighbours[f : f + 1, :].astype(F32))
        pick[f * 256 : (f + 1) * 256, :] = jnp.where(lanes == names, 1.0, 0.0).astype(BF16)
        target = jnp.where(lane // 32 == f, lane % 32 + 256, -1).astype(F32)
        halo_hit = halo_hit + jnp.where(target == names, 1.0, 0.0)
    halo_hit = halo_hit.astype(BF16)
    halo_pick[...] = halo_hit
    halo_sent = dot(choose, halo_hit).astype(BF16)

    def faces(parts):
        for f in range(4):
            rows = dot(pick[f * 256 : (f + 1) * 256, :], parts)
            gathered[:, f * 256 : (f + 1) * 256] = rows.astype(BF16)
        return halves(dot(gathered[...], face_w[...]))

    def timed(parts):
        return halves(dot(parts, time_w[...]))

    def halo_parts(rows):
        parts = split(rows)
        each = [halves(dot(parts, face_w[f * 256 : (f + 1) * 256, :])) for f in range(4)]
        return split(jnp.concatenate(each, axis=0))

    def chosen(x):
        return halves(dot(choose, split(x)))

    base1 = 1.3 * v0_1 + sigma * (faces(s1) + timed(s0))
    base0 = 1.3 * v0_0 + sigma * faces(s0)
    sent_base1 = chosen(base1)
    sent_base0 = chosen(base0)
    for copy in first_halo + [first_sent]:
        copy.wait()
    started = k > 0
    h0 = halo_parts(halo0[0])
    h1 = halo_parts(halo0[1])
    early = jnp.where(started, before_sent[...], 0.0)
    v1_sent[0] = sent_base0 + sent_sigma * (halves(dot(halo_sent, h0)) + timed(split(early)))
    v1_sent[1] = sent_base1 + sent_sigma * halves(dot(halo_sent, h1))
    second_halo = halo_copies(v1_sent, halo1, 4)
    for copy in second_halo:
        copy.start()
    v1_1 = base1 + sigma * halves(dot(halo_pick[...], h1))
    base0 = base0 + sigma * halves(dot(halo_pick[...], h0))
    r1 = a1 - scale * v1_1 + faces(split(v1_1))
    first_last.wait()
    v1_0 = base0 + sigma * timed(split(jnp.where(started, before0[...], 0.0)))
    s0 = split(v1_0)
    r1 = r1 + timed(s0)
    total = r1 + a0 - scale * v1_0 + faces(s0)
    for copy in second_halo:
        copy.wait()
    h1 = halo1[1]
    both = halo_parts(halo1[0] + h1)
    total = total + halves(dot(halo_pick[...], both))
    rhs[...] = coarse * total + v1_1
    mine = pl.ds(pl.multiple_of(k * 16, 16), 16)

    def exchange(src, dst, number):
        for other in others:
            theirs = pl.ds(pl.multiple_of(other * 16, 16), 16)
            remote(src.at[theirs], dst.at[mine], number, {"tm": other}).start()
        count = pl.ds(0, 16 * (groups - 1))
        return remote(src.at[count], dst.at[count], number, after)

    to_owners = exchange(rhs, rhs_all, 6)
    rhs_all[mine, :] = rhs[mine, :]
    r1 = r1 + halves(dot(halo_pick[...], halo_parts(h1)))
    step = r1 * sigma
    pre0 = v1_0 - step
    pre1 = step

    m2 = halves(dot(split(m1), w1))
    w2 = weights(m2)
    m34 = halves(dot(split(jnp.concatenate([m1, m2], axis=0)), w2))
    m3, m4 = m34[:128], m34[128:]
    w4 = weights(m4)
    m8 = halves(dot(split(m4), w4))
    m12 = halves(dot(split(m8), w4))
    for i, w in enumerate([w1, w2, weights(m3)]):
        near_w[:, i * 256 : (i + 1) * 256] = w
    for i, w in enumerate([w4, weights(m8), weights(m12)]):
        far_w[:, i * 256 : (i + 1) * 256] = w
    own_scale = scale_full[mine, :]
    own_scale = 1.0 / (2.0 * own_scale - 1.0)
    c1 = jnp.concatenate([own_scale] * groups, axis=0)
    c2 = c1 * c1
    c4 = c2 * c2
    c8 = c4 * c4

    to_owners.wait()
    x = rhs_all[...]
    y = dot(split(x), near_w[...])
    x = (
        x
        + later(c1 * halves(y[:, 0:256]), 1)
        + later(c2 * halves(y[:, 256:512]), 2)
        + later(c1 * c2 * halves(y[:, 512:768]), 3)
    )
    y = dot(split(x), far_w[...])
    x = (
        x
        + later(c4 * halves(y[:, 0:256]), 4)
        + later(c8 * halves(y[:, 256:512]), 8)
        + later(c4 * c8 * halves(y[:, 512:768]), 12)
    )
    chain_out[...] = x
    to_slabs = exchange(chain_out, chain_all, 7)
    chain_all[mine, :] = chain_out[mine, :]
    to_slabs.wait()

    w = chain_all[...]
    c = w - v1_1
    sc = split(c)
    c_sent[...] = halves(dot(choose, sc))
    third_halo = halo_copies(c_sent, halo_c, 8)
    for copy in third_halo:
        copy.start()
    fc = faces(sc)
    base0 = pre0 + (1.0 + DAMPING - sigma) * c + sigma * fc
    base1 = w + pre1 - DAMPING * c + sigma * (fc + timed(sc))
    sent_base0 = chosen(base0)
    sent_base1 = chosen(base1)
    for copy in third_halo:
        copy.wait()
    hc = halo_parts(halo_c[...])
    extra = sent_sigma * halves(dot(halo_sent, hc))
    v3_sent[0] = sent_base0 + extra
    v3_sent[1] = sent_base1 + extra
    fourth_halo = halo_copies(v3_sent, halo3, 10)
    for copy in fourth_halo:
        copy.start()
    extra = sigma * halves(dot(halo_pick[...], hc))
    v3_1 = base1 + extra
    v3_last[...] = v3_1
    last = remote(v3_last, before3, 12, after)
    last.start()
    v3_0 = base0 + extra
    s0 = split(v3_0)
    s1 = split(v3_1)
    u1 = faces(s1) + timed(s0)
    u0 = faces(s0)
    for copy in fourth_halo:
        copy.wait()
    u1 = u1 + halves(dot(halo_pick[...], halo_parts(halo3[1])))
    out_ref[1] = v0_last[...] + (1.0 - DAMPING) * v3_1 + sigma * u1
    u0 = u0 + halves(dot(halo_pick[...], halo_parts(halo3[0])))
    base0 = sigma * a0 + (1.0 - DAMPING) * v3_0 + sigma * u0
    last.wait()
    out_ref[0] = base0 + sigma * timed(split(jnp.where(started, before3[...], 0.0)))


def solution(mesh):
    groups, partitions = mesh.shape["tm"], mesh.shape["space"]

    def body(source, elem_scale, diag_block, block_inverse, face_flux, time_trace, neighbours, send_rows):
        any_space = pl.BlockSpec(memory_space=pl.ANY)
        vmem = pltpu.VMEM
        rows = (256, 128)
        return pl.pallas_call(
            lambda *refs: kernel(groups, partitions, *refs),
            out_shape=jax.ShapeDtypeStruct((2, 256, 128), F32),
            in_specs=[any_space] * 7,
            out_specs=pl.BlockSpec(memory_space=pltpu.VMEM),
            scratch_shapes=[
                vmem((2, 256, 128), F32), vmem((1, 256), F32), vmem((128, 128), F32), vmem((4, 128, 128), F32),
                vmem((128, 128), F32), vmem((4, 256), jnp.int32), vmem((1, 32), jnp.int32),
                vmem((1024, 256), BF16), vmem((256, 128), BF16), vmem((1024, 256), BF16), vmem((256, 256), BF16),
                vmem((256, 768), BF16), vmem((256, 768), BF16), vmem((256, 1024), BF16),
                vmem(rows, F32), vmem((2, 32, 128), F32), vmem((2, 32, 128), F32), vmem((32, 128), F32),
                vmem((2, 32, 128), F32), vmem(rows, F32),
                vmem((2, 32, 128), F32), vmem((2, 32, 128), F32), vmem((32, 128), F32), vmem((2, 32, 128), F32),
                vmem(rows, F32), vmem((32, 128), F32), vmem(rows, F32),
                vmem(rows, F32), vmem(rows, F32), vmem(rows, F32), vmem(rows, F32), vmem(rows, F32),
                pltpu.SemaphoreType.DMA((7,)), pltpu.SemaphoreType.DMA((13,)), pltpu.SemaphoreType.DMA((13,)),
            ],
            compiler_params=pltpu.CompilerParams(
                collective_id=0, has_side_effects=True, vmem_limit_bytes=32 * 1024 * 1024
            ),
        )(source, elem_scale.reshape(1, 256), block_inverse, face_flux, time_trace, neighbours.T, send_rows)

    return jax.shard_map(
        body,
        mesh=mesh,
        in_specs=(P("tm", "space", None), P("space"), P(), P(), P(), P(), P("space", None), P("space", None)),
        out_specs=P("tm", "space", None),
        check_vma=False,
    )
```

```python
import jax
import jax.numpy as jnp
from jax import lax
from jax.experimental import pallas as pl
from jax.experimental.pallas import tpu as pltpu
from jax.sharding import PartitionSpec as P

DAMPING = 0.7
KEEP = 1.0 - DAMPING
F32 = jnp.float32
BF16 = jnp.bfloat16
MESH = pl.DeviceIdType.MESH


def dot(left, right):
    return jnp.dot(left, right, preferred_element_type=F32)


def split(x):
    high = x.astype(BF16)
    low = (x - high.astype(F32)).astype(BF16)
    return jnp.concatenate([high, low], axis=1)


def halves(x):
    width = x.shape[1] // 2
    return x[:, :width] + x[:, width:]


def weights(matrix):
    parts = split(matrix)
    return jnp.concatenate([parts, parts], axis=0)


def iota(shape, dim):
    return lax.broadcasted_iota(jnp.int32, shape, dim)


def column(row):
    size = row.shape[1]
    same = iota((size, size), 0) == iota((size, size), 1)
    return jnp.sum(jnp.where(same, row, 0.0), axis=1, keepdims=True)


def onehot(hit):
    return jnp.where(hit, 1.0, 0.0).astype(BF16)


def any_hit(hits):
    total = jnp.where(hits[0], 1.0, 0.0)
    for hit in hits[1:]:
        total = total + jnp.where(hit, 1.0, 0.0)
    return total.astype(BF16)


def later(blocks, by):
    zeros = jnp.zeros((16 * by, blocks.shape[1]), F32)
    return jnp.concatenate([zeros, blocks[: -16 * by]], axis=0)


def kernel(
    groups, partitions,
    source_hbm, scale_hbm, inverse_hbm, flux_hbm, trace_hbm, neighbours_hbm, send_hbm,
    out_ref,
    source, scale_row, inverse, flux, trace, neighbours, send_row,
    pick, spread, face_w, near_w, far_w, gathered,
    v0_last, out1, in1, far1, diag1, before0,
    rhs, rhs_all, carry, before_carry, chain_out, chain_all, out3, in3, far3, scale_full,
    in_sem, send_sem, recv_sem,
):
    k = lax.axis_index("tm")
    p = lax.axis_index("space")
    loads = [
        pltpu.make_async_copy(src, dst, in_sem.at[i])
        for i, (src, dst) in enumerate(
            [
                (scale_hbm, scale_row), (send_hbm, send_row), (neighbours_hbm, neighbours), (inverse_hbm, inverse),
                (source_hbm, source), (flux_hbm, flux), (trace_hbm, trace),
            ]
        )
    ]
    for load in loads:
        load.start()

    def space(by):
        return lax.rem(p + partitions + by, partitions)

    others = []
    for hops in (4, 3, 2, 1):
        for dy in range(4):
            for dx in range(4):
                if min(dy, 4 - dy) + min(dx, 4 - dx) == hops:
                    others.append(lax.rem(k // 4 + dy, 4) * 4 + lax.rem(lax.rem(k, 4) + dx, 4))
    after = lax.rem(k + 1, groups)
    ahead = lax.rem(k + groups - 1, groups)

    barrier = pltpu.get_barrier_semaphore()
    senders = [{"tm": other} for other in others]
    senders += [{"space": space(by)} for by in (1, -1, 2, -2)]
    senders += [{"tm": ahead, "space": space(by)} for by in (1, -1)]
    for partner in senders:
        pl.semaphore_signal(barrier, inc=1, device_id=partner, device_id_type=MESH)

    def remote(src, dst, number, device):
        return pltpu.make_async_remote_copy(
            src_ref=src, dst_ref=dst, send_sem=send_sem.at[number], recv_sem=recv_sem.at[number],
            device_id=device, device_id_type=MESH,
        )

    for load in loads[:3]:
        load.wait()
    scale = column(scale_row[...])
    scale_full[...] = jnp.broadcast_to(scale, (256, 128))
    sigma = DAMPING / scale
    coarse = 1.0 / (2.0 * scale - 1.0)
    send_f = send_row[...].astype(F32)
    send_col = column(send_f)
    lanes = iota((256, 256), 1).astype(F32)
    choose_hit = iota((32, 256), 1).astype(F32) == send_col
    choose = onehot(choose_hit)
    sent_scale = jnp.sum(jnp.where(choose_hit, scale_row[...], 0.0), axis=1, keepdims=True)
    sent_sigma = DAMPING / sent_scale
    name_rows = [neighbours[f : f + 1, :].astype(F32) for f in range(4)]
    sent_names = [jnp.sum(jnp.where(choose_hit, row, 0.0), axis=1, keepdims=True) for row in name_rows]
    wide = iota((32, 256), 1).astype(F32)
    sent_pick = jnp.concatenate([onehot(wide == names) for names in sent_names], axis=0)

    def halo_hits(names, size):
        lane = iota((size, 128), 1)
        hits = []
        for f in range(4):
            target = jnp.where(lane // 32 == f, lane % 32 + 256, -1).astype(F32)
            hits.append(target == names[f])
        return any_hit(hits)

    halo_sent = halo_hits(sent_names, 32)
    lane = iota((32, 128), 1)
    facts = jnp.where(lane == 4, sent_sigma, 0.0)
    for f in range(4):
        facts = facts + jnp.where(lane == f, sent_names[f], 0.0)
    out1[4] = facts

    loads[3].wait()
    inverse_w = weights(inverse[...])
    loads[4].wait()
    v0_0 = sigma * halves(dot(split(source[0]), inverse_w))
    v0_1 = sigma * halves(dot(split(source[1]), inverse_w))
    v0_last[...] = v0_1
    a0 = v0_0 * scale * (1.0 / DAMPING)
    a1 = v0_1 * scale * (1.0 / DAMPING)
    for load in loads[5:]:
        load.wait()
    flux_b = halves(dot(split(flux[...].reshape(512, 128)), inverse_w))
    for f in range(4):
        face_w[f * 256 : (f + 1) * 256, :] = weights(flux_b[f * 128 : (f + 1) * 128])
    m1 = halves(dot(split(trace[...]), inverse_w))
    w1 = weights(m1)
    near_w[:, 0:256] = w1
    s0 = split(v0_0)
    s1 = split(v0_1)
    own0 = halves(dot(choose, s0))
    own1 = halves(dot(choose, s1))
    out1[0] = own0
    out1[1] = own1

    def timed(x):
        return halves(dot(split(x), near_w[:, 0:256]))

    def sent_faces(parts):
        rows = dot(sent_pick, parts).astype(BF16)
        rows = jnp.concatenate([rows[f * 32 : (f + 1) * 32] for f in range(4)], axis=1)
        return halves(dot(rows, face_w[...]))

    out1[2] = (1.0 + KEEP) * own0 + sent_sigma * sent_faces(s0)
    out1[3] = (1.0 + KEEP) * own1 + sent_sigma * (sent_faces(s1) + timed(own0))
    pl.semaphore_wait(barrier, groups + 5)

    to_right, to_left = pl.ds(16, 16), pl.ds(0, 16)
    first = [
        remote(out1.at[:, to_right], in1.at[:, to_left], 0, {"space": space(1)}),
        remote(out1.at[:, to_left], in1.at[:, to_right], 1, {"space": space(-1)}),
        remote(out1.at[0:2, to_right], far1.at[:, to_left], 2, {"space": space(2)}),
        remote(out1.at[0:2, to_left], far1.at[:, to_right], 3, {"space": space(-2)}),
        remote(out1.at[1, to_right], diag1.at[to_left], 4, {"tm": after, "space": space(1)}),
        remote(out1.at[1, to_left], diag1.at[to_right], 5, {"tm": after, "space": space(-1)}),
    ]
    first_last = remote(v0_last, before0, 6, {"tm": after})
    for copy in first + [first_last]:
        copy.start()

    send4 = jnp.concatenate([send_col] * 4, axis=0)
    eye = iota((128, 128), 0) == iota((128, 128), 1)
    send4 = jnp.sum(jnp.where(eye, send4, 0.0), axis=0, keepdims=True)
    names = [column(row) for row in name_rows]
    for f in range(4):
        pick[f * 256 : (f + 1) * 256, :] = onehot(lanes == names[f])
    spread[:, 0:128] = halo_hits(names, 256)
    lane = iota((256, 128), 1)
    spread[:, 128:256] = any_hit([(jnp.where(lane // 32 == f, send4, -1.0) == names[f]) for f in range(4)])
    element = iota((256, 128), 0).astype(F32)
    spread[:, 256:384] = onehot(jnp.where(lane < 32, send4, -1.0) == element)

    def gather(parts, ref):
        for f in range(4):
            rows = dot(pick[f * 256 : (f + 1) * 256, :], parts)
            ref[:, f * 256 : (f + 1) * 256] = rows.astype(BF16)
        return halves(dot(ref[...], face_w[...]))

    def faces(x):
        return gather(split(x), gathered)

    def stacks(rows):
        parts = split(rows)
        each = [halves(dot(parts, face_w[f * 256 : (f + 1) * 256, :])) for f in range(4)]
        count = rows.shape[0] // 32
        return [jnp.concatenate([e[i * 32 : (i + 1) * 32] for e in each], axis=0) for i in range(count)]

    def scattered(halo_stack, change_stack, own_rows):
        rest = jnp.zeros((96, 128), F32)
        right = jnp.concatenate([halo_stack, change_stack, own_rows, rest], axis=0)
        return halves(dot(spread[...], split(right)))

    def chosen(x):
        return halves(dot(choose, split(x)))

    base1 = (1.0 + KEEP) * v0_1 + sigma * (gather(s1, gathered) + timed(v0_0))
    base0 = (1.0 + KEEP) * v0_0 + sigma * gather(s0, gathered)
    rest1 = a1 - scale * base1 + faces(base1) + timed(base0)
    rest0 = a0 - scale * base0 + faces(base0)

    for copy in first:
        copy.wait()
    started = k > 0
    facts = in1[4]
    far_names = [facts[:, f : f + 1] for f in range(4)]
    halo_sigma = facts[:, 4:5]
    far_hits = halo_hits(far_names, 32).astype(F32)
    upper = iota((32, 128), 0) < 16
    far_halo = jnp.concatenate([jnp.where(upper, far_hits, 0.0), jnp.where(upper, 0.0, far_hits)], axis=1).astype(BF16)

    def seen_by_halo(far, own):
        return [far[0:16], own[0:16], own[16:32], far[16:32]]

    st = stacks(
        jnp.concatenate([in1[0], in1[1]] + seen_by_halo(far1[0], own0) + seen_by_halo(far1[1], own1), axis=0)
    )
    change0 = sent_sigma * halves(dot(halo_sent, split(st[0])))
    change1 = sent_sigma * halves(dot(halo_sent, split(st[1])))
    halo_v0 = in1[2] + halo_sigma * (
        halves(dot(far_halo, split(jnp.concatenate(st[2:4], axis=0)))) + timed(jnp.where(started, diag1[...], 0.0))
    )
    halo_v1 = in1[3] + halo_sigma * halves(dot(far_halo, split(jnp.concatenate(st[4:6], axis=0))))
    st = stacks(jnp.concatenate([halo_v0, halo_v1, change0, change1], axis=0))
    rest1 = rest1 + scattered(st[1], st[3], timed(change0) - sent_scale * change1)
    rest0 = rest0 + scattered(st[0], st[2], -sent_scale * change0)
    place = spread[:, 256:384]
    rest = jnp.zeros((96, 128), F32)
    v1_1 = base1 + halves(dot(place, split(jnp.concatenate([change1, rest], axis=0))))
    base0 = base0 + halves(dot(place, split(jnp.concatenate([change0, rest], axis=0))))
    ready = coarse * (rest0 + rest1) + v1_1

    first_last.wait()
    delta = sigma * timed(jnp.where(started, before0[...], 0.0))
    t_delta = timed(delta)
    rhs[...] = ready + coarse * (faces(delta) + t_delta - scale * delta)
    mine = pl.ds(pl.multiple_of(k * 16, 16), 16)

    def block(i, size=16):
        return pl.ds(pl.multiple_of(i * 16, 16), size)

    for other in others:
        remote(rhs.at[block(other)], rhs_all.at[mine], 7, {"tm": other}).start()
    count = pl.ds(0, 16 * (groups - 1))
    to_owners = remote(rhs.at[count], rhs_all.at[count], 7, {"tm": after})
    rhs_all[mine, :] = rhs[mine, :]

    v1_0 = base0 + delta
    step = sigma * (rest1 + t_delta)
    carry[...] = v0_1 + sigma * timed(v1_0 - v1_1)
    carried = remote(carry, before_carry, 8, {"tm": after})
    carried.start()
    pre0 = v1_0 - step
    pre1 = v1_1 + step
    sent_pre0 = chosen(pre0)
    sent_pre1 = chosen(pre1)
    pre1 = step

    m2 = halves(dot(split(m1), w1))
    w2 = weights(m2)
    m34 = halves(dot(split(jnp.concatenate([m1, m2], axis=0)), w2))
    m3, m4 = m34[:128], m34[128:]
    w4 = weights(m4)
    m8 = halves(dot(split(m4), w4))
    m12 = halves(dot(split(m8), w4))
    near_w[:, 256:512] = w2
    near_w[:, 512:768] = weights(m3)
    for i, w in enumerate([w4, weights(m8), weights(m12)]):
        far_w[:, i * 256 : (i + 1) * 256] = w
    own_scale = scale_full[mine, :]
    own_scale = 1.0 / (2.0 * own_scale - 1.0)
    c1 = jnp.concatenate([own_scale] * groups, axis=0)
    c2 = c1 * c1
    c4 = c2 * c2
    c8 = c4 * c4
    chain_out[0:16, :] = jnp.zeros((16, 128), F32)

    to_owners.wait()
    x = rhs_all[...]
    y = dot(split(x), near_w[...])
    x = (
        x
        + later(c1 * halves(y[:, 0:256]), 1)
        + later(c2 * halves(y[:, 256:512]), 2)
        + later(c1 * c2 * halves(y[:, 512:768]), 3)
    )
    y = dot(split(x), far_w[...])
    chain_out[16:272, :] = (
        x
        + later(c4 * halves(y[:, 0:256]), 4)
        + later(c8 * halves(y[:, 256:512]), 8)
        + later(c4 * c8 * halves(y[:, 512:768]), 12)
    )
    for other in others:
        remote(chain_out.at[block(other, 32)], chain_all.at[k], 9, {"tm": other}).start()
    to_slabs = remote(chain_all.at[pl.ds(0, groups - 1)], chain_all.at[pl.ds(0, groups - 1)], 9, {"tm": after})
    chain_all[k] = chain_out[block(k, 32), :]
    for copy in (to_slabs, carried):
        copy.wait()

    w = chain_all[:, 16:32].reshape(256, 128)
    wp = chain_all[:, 0:16].reshape(256, 128)
    c = w - v1_1
    sc = split(c)
    sp = split(wp)
    sent_c = halves(dot(choose, sc))
    sent_fc = sent_faces(sc)
    out3[0] = sent_c
    out3[1] = halves(dot(choose, sp))
    out3[2] = sent_pre0 + (1.0 + DAMPING - sent_sigma) * sent_c + sent_sigma * sent_fc
    out3[3] = sent_pre1 + KEEP * sent_c + sent_sigma * (sent_fc + timed(sent_c))
    second = [
        remote(out3.at[:, to_right], in3.at[:, to_left], 10, {"space": space(1)}),
        remote(out3.at[:, to_left], in3.at[:, to_right], 11, {"space": space(-1)}),
        remote(out3.at[0, to_right], far3.at[to_left], 12, {"space": space(2)}),
        remote(out3.at[0, to_left], far3.at[to_right], 13, {"space": space(-2)}),
    ]
    for copy in second:
        copy.start()

    fc = gather(sc, gathered)
    base0 = pre0 + (1.0 + DAMPING - sigma) * c + sigma * fc
    base1 = w + pre1 - DAMPING * c + sigma * (fc + timed(c))
    basep = before_carry[...] + KEEP * wp + sigma * (gather(sp, gathered) + timed(wp))
    basep = jnp.where(started, basep, 0.0)
    base1 = v0_1 + KEEP * base1 + sigma * (faces(base1) + timed(base0))
    base0 = v0_0 + KEEP * base0 + sigma * (faces(base0) + timed(basep))

    for copy in second:
        copy.wait()
    st = stacks(jnp.concatenate([in3[0], in3[1]] + seen_by_halo(far3[...], sent_c), axis=0))
    seen = halves(dot(halo_sent, split(st[0])))
    change = sent_sigma * seen
    change_p = sent_sigma * halves(dot(halo_sent, split(st[1])))
    extra = halo_sigma * halves(dot(far_halo, split(jnp.concatenate(st[2:4], axis=0))))
    st = stacks(jnp.concatenate([in3[2] + extra, in3[3] + extra, change], axis=0))
    t = timed(jnp.concatenate([change, change_p], axis=0))
    kept = KEEP * seen
    out_ref[1] = base1 + sigma * scattered(st[1], st[2], kept + t[0:32])
    out_ref[0] = base0 + sigma * scattered(st[0], st[2], kept + t[32:64])


def solution(mesh):
    groups, partitions = mesh.shape["tm"], mesh.shape["space"]

    def body(source, elem_scale, diag_block, block_inverse, face_flux, time_trace, neighbours, send_rows):
        any_space = pl.BlockSpec(memory_space=pl.ANY)
        vmem = pltpu.VMEM
        rows = (256, 128)
        return pl.pallas_call(
            lambda *refs: kernel(groups, partitions, *refs),
            out_shape=jax.ShapeDtypeStruct((2, 256, 128), F32),
            in_specs=[any_space] * 7,
            out_specs=pl.BlockSpec(memory_space=pltpu.VMEM),
            scratch_shapes=[
                vmem((2, 256, 128), F32), vmem((1, 256), F32), vmem((128, 128), F32), vmem((4, 128, 128), F32),
                vmem((128, 128), F32), vmem((4, 256), jnp.int32), vmem((1, 32), jnp.int32),
                vmem((1024, 256), BF16), vmem((256, 384), BF16), vmem((1024, 256), BF16),
                vmem((256, 768), BF16), vmem((256, 768), BF16), vmem((256, 1024), BF16),
                vmem(rows, F32), vmem((5, 32, 128), F32), vmem((5, 32, 128), F32), vmem((2, 32, 128), F32),
                vmem((32, 128), F32), vmem(rows, F32),
                vmem(rows, F32), vmem(rows, F32), vmem(rows, F32), vmem(rows, F32),
                vmem((16 * (groups + 1), 128), F32), vmem((groups, 32, 128), F32),
                vmem((4, 32, 128), F32), vmem((4, 32, 128), F32), vmem((32, 128), F32), vmem(rows, F32),
                pltpu.SemaphoreType.DMA((7,)), pltpu.SemaphoreType.DMA((14,)), pltpu.SemaphoreType.DMA((14,)),
            ],
            compiler_params=pltpu.CompilerParams(
                collective_id=0, has_side_effects=True, vmem_limit_bytes=56 * 1024 * 1024
            ),
        )(source, elem_scale.reshape(1, 256), block_inverse, face_flux, time_trace, neighbours.T, send_rows)

    return jax.shard_map(
        body,
        mesh=mesh,
        in_specs=(P("tm", "space", None), P("space"), P(), P(), P(), P(), P("space", None), P("space", None)),
        out_specs=P("tm", "space", None),
        check_vma=False,
    )
```

```python
import jax
import jax.numpy as jnp
from jax import lax
from jax.experimental import pallas as pl
from jax.experimental.pallas import tpu as pltpu
from jax.sharding import PartitionSpec as P

DAMPING = 0.7
KEEP = 1.0 - DAMPING
F32 = jnp.float32
BF16 = jnp.bfloat16
MESH = pl.DeviceIdType.MESH


def dot(left, right):
    return jnp.dot(left, right, preferred_element_type=F32)


def split(x):
    high = x.astype(BF16)
    low = (x - high.astype(F32)).astype(BF16)
    return jnp.concatenate([high, low], axis=1)


def halves(x):
    width = x.shape[1] // 2
    return x[:, :width] + x[:, width:]


def weights(matrix):
    parts = split(matrix)
    return jnp.concatenate([parts, parts], axis=0)


def iota(shape, dim):
    return lax.broadcasted_iota(jnp.int32, shape, dim)


def column(row):
    size = row.shape[1]
    same = iota((size, size), 0) == iota((size, size), 1)
    return jnp.sum(jnp.where(same, row, 0.0), axis=1, keepdims=True)


def onehot(hit):
    return jnp.where(hit, 1.0, 0.0).astype(BF16)


def any_hit(hits):
    total = jnp.where(hits[0], 1.0, 0.0)
    for hit in hits[1:]:
        total = total + jnp.where(hit, 1.0, 0.0)
    return total.astype(BF16)


def later(blocks, by):
    zeros = jnp.zeros((16 * by, blocks.shape[1]), F32)
    return jnp.concatenate([zeros, blocks[: -16 * by]], axis=0)


def kernel(
    groups, partitions,
    source_hbm, scale_hbm, inverse_hbm, flux_hbm, trace_hbm, neighbours_hbm, send_hbm,
    out_ref,
    source, scale_row, inverse, flux, trace, neighbours, send_row,
    pick, spread, face_w, near_w, far_w, gathered,
    v0_last, out1, in1, far1, before0,
    rhs, rhs_all, carry, before_carry, chain_out, chain_all, out3, in3, far3, scale_full,
    in_sem, send_sem, recv_sem,
):
    k = lax.axis_index("tm")
    p = lax.axis_index("space")
    loads = [
        pltpu.make_async_copy(src, dst, in_sem.at[i])
        for i, (src, dst) in enumerate(
            [
                (scale_hbm, scale_row), (send_hbm, send_row), (neighbours_hbm, neighbours), (inverse_hbm, inverse),
                (source_hbm, source), (flux_hbm, flux), (trace_hbm, trace),
            ]
        )
    ]
    for load in loads:
        load.start()

    def space(by):
        return lax.rem(p + partitions + by, partitions)

    others = []
    for hops in (4, 3, 2, 1):
        for dy in range(4):
            for dx in range(4):
                if min(dy, 4 - dy) + min(dx, 4 - dx) == hops:
                    others.append(lax.rem(k // 4 + dy, 4) * 4 + lax.rem(lax.rem(k, 4) + dx, 4))
    after = lax.rem(k + 1, groups)

    barrier = pltpu.get_barrier_semaphore()
    senders = [{"tm": other} for other in others]
    senders += [{"space": space(by)} for by in (1, -1, 2, -2)]
    for partner in senders:
        pl.semaphore_signal(barrier, inc=1, device_id=partner, device_id_type=MESH)

    def remote(src, dst, number, device):
        return pltpu.make_async_remote_copy(
            src_ref=src, dst_ref=dst, send_sem=send_sem.at[number], recv_sem=recv_sem.at[number],
            device_id=device, device_id_type=MESH,
        )

    for load in loads[:3]:
        load.wait()
    scale = column(scale_row[...])
    scale_full[...] = jnp.broadcast_to(scale, (256, 128))
    sigma = DAMPING / scale
    coarse = 1.0 / (2.0 * scale - 1.0)
    send_f = send_row[...].astype(F32)
    send_col = column(send_f)
    lanes = iota((256, 256), 1).astype(F32)
    choose_hit = iota((32, 256), 1).astype(F32) == send_col
    choose = onehot(choose_hit)
    sent_scale = jnp.sum(jnp.where(choose_hit, scale_row[...], 0.0), axis=1, keepdims=True)
    sent_sigma = DAMPING / sent_scale
    name_rows = [neighbours[f : f + 1, :].astype(F32) for f in range(4)]
    sent_names = [jnp.sum(jnp.where(choose_hit, row, 0.0), axis=1, keepdims=True) for row in name_rows]
    wide = iota((32, 256), 1).astype(F32)
    sent_pick = jnp.concatenate([onehot(wide == names) for names in sent_names], axis=0)

    def halo_hits(names, size):
        lane = iota((size, 128), 1)
        hits = []
        for f in range(4):
            target = jnp.where(lane // 32 == f, lane % 32 + 256, -1).astype(F32)
            hits.append(target == names[f])
        return any_hit(hits)

    halo_sent = halo_hits(sent_names, 32)
    lane = iota((32, 128), 1)
    facts = jnp.where(lane == 4, sent_sigma, 0.0)
    for f in range(4):
        facts = facts + jnp.where(lane == f, sent_names[f], 0.0)
    out1[4] = facts

    loads[3].wait()
    inverse_w = weights(inverse[...])
    loads[4].wait()
    v0_0 = sigma * halves(dot(split(source[0]), inverse_w))
    v0_1 = sigma * halves(dot(split(source[1]), inverse_w))
    v0_last[...] = v0_1
    a0 = v0_0 * scale * (1.0 / DAMPING)
    a1 = v0_1 * scale * (1.0 / DAMPING)
    for load in loads[5:]:
        load.wait()
    flux_b = halves(dot(split(flux[...].reshape(512, 128)), inverse_w))
    for f in range(4):
        face_w[f * 256 : (f + 1) * 256, :] = weights(flux_b[f * 128 : (f + 1) * 128])
    m1 = halves(dot(split(trace[...]), inverse_w))
    w1 = weights(m1)
    near_w[:, 0:256] = w1
    s0 = split(v0_0)
    s1 = split(v0_1)
    own0 = halves(dot(choose, s0))
    own1 = halves(dot(choose, s1))
    out1[0] = own0
    out1[1] = own1

    def timed(x):
        return halves(dot(split(x), near_w[:, 0:256]))

    def sent_faces(parts):
        rows = dot(sent_pick, parts).astype(BF16)
        rows = jnp.concatenate([rows[f * 32 : (f + 1) * 32] for f in range(4)], axis=1)
        return halves(dot(rows, face_w[...]))

    out1[2] = (1.0 + KEEP) * own0 + sent_sigma * sent_faces(s0)
    out1[3] = (1.0 + KEEP) * own1 + sent_sigma * (sent_faces(s1) + timed(own0))
    pl.semaphore_wait(barrier, groups + 3)

    to_right, to_left = pl.ds(16, 16), pl.ds(0, 16)
    first = [
        remote(out1.at[:, to_right], in1.at[:, to_left], 0, {"space": space(1)}),
        remote(out1.at[:, to_left], in1.at[:, to_right], 1, {"space": space(-1)}),
        remote(out1.at[0:2, to_right], far1.at[:, to_left], 2, {"space": space(2)}),
        remote(out1.at[0:2, to_left], far1.at[:, to_right], 3, {"space": space(-2)}),
    ]
    first_last = remote(v0_last, before0, 4, {"tm": after})
    for copy in first + [first_last]:
        copy.start()

    send4 = jnp.concatenate([send_col] * 4, axis=0)
    eye = iota((128, 128), 0) == iota((128, 128), 1)
    send4 = jnp.sum(jnp.where(eye, send4, 0.0), axis=0, keepdims=True)
    names = [column(row) for row in name_rows]
    for f in range(4):
        pick[f * 256 : (f + 1) * 256, :] = onehot(lanes == names[f])
    spread[:, 0:128] = halo_hits(names, 256)
    lane = iota((256, 128), 1)
    spread[:, 128:256] = any_hit([(jnp.where(lane // 32 == f, send4, -1.0) == names[f]) for f in range(4)])
    element = iota((256, 128), 0).astype(F32)
    spread[:, 256:384] = onehot(jnp.where(lane < 32, send4, -1.0) == element)

    def gather(parts, ref):
        for f in range(4):
            rows = dot(pick[f * 256 : (f + 1) * 256, :], parts)
            ref[:, f * 256 : (f + 1) * 256] = rows.astype(BF16)
        return halves(dot(ref[...], face_w[...]))

    def faces(x):
        return gather(split(x), gathered)

    def stacks(rows):
        parts = split(rows)
        each = [halves(dot(parts, face_w[f * 256 : (f + 1) * 256, :])) for f in range(4)]
        count = rows.shape[0] // 32
        return [jnp.concatenate([e[i * 32 : (i + 1) * 32] for e in each], axis=0) for i in range(count)]

    def scattered(halo_stack, change_stack, own_rows):
        rest = jnp.zeros((96, 128), F32)
        right = jnp.concatenate([halo_stack, change_stack, own_rows, rest], axis=0)
        return halves(dot(spread[...], split(right)))

    def chosen(x):
        return halves(dot(choose, split(x)))

    base1 = (1.0 + KEEP) * v0_1 + sigma * (gather(s1, gathered) + timed(v0_0))
    base0 = (1.0 + KEEP) * v0_0 + sigma * gather(s0, gathered)
    rest1 = a1 - scale * base1 + faces(base1) + timed(base0)
    rest0 = a0 - scale * base0 + faces(base0)
    onward = sigma * timed(v0_1)
    onward = faces(onward) + timed(onward) - scale * onward

    for copy in first:
        copy.wait()
    started = k > 0
    facts = in1[4]
    far_names = [facts[:, f : f + 1] for f in range(4)]
    halo_sigma = facts[:, 4:5]
    far_hits = halo_hits(far_names, 32).astype(F32)
    upper = iota((32, 128), 0) < 16
    far_halo = jnp.concatenate([jnp.where(upper, far_hits, 0.0), jnp.where(upper, 0.0, far_hits)], axis=1).astype(BF16)

    def seen_by_halo(far, own):
        return [far[0:16], own[0:16], own[16:32], far[16:32]]

    st = stacks(
        jnp.concatenate([in1[0], in1[1]] + seen_by_halo(far1[0], own0) + seen_by_halo(far1[1], own1), axis=0)
    )
    change0 = sent_sigma * halves(dot(halo_sent, split(st[0])))
    change1 = sent_sigma * halves(dot(halo_sent, split(st[1])))
    halo_v0 = in1[2] + halo_sigma * halves(dot(far_halo, split(jnp.concatenate(st[2:4], axis=0))))
    halo_v1 = in1[3] + halo_sigma * halves(dot(far_halo, split(jnp.concatenate(st[4:6], axis=0))))
    change = change0 + change1
    t_change0 = timed(change0)
    st = stacks(jnp.concatenate([halo_v0 + halo_v1, change, halo_sigma * timed(in1[1])], axis=0))
    total = rest0 + rest1 + scattered(st[0], st[1], t_change0 - sent_scale * change)
    onward = onward + halves(dot(spread[:, 0:128], split(st[2])))
    place = spread[:, 256:384]
    rest = jnp.zeros((96, 128), F32)
    v1_1 = base1 + halves(dot(place, split(jnp.concatenate([change1, rest], axis=0))))
    rhs[:, 0:16] = (coarse * total + v1_1).reshape(groups, 16, 128)
    rhs[:, 16:32] = (coarse * onward).reshape(groups, 16, 128)
    mine = pl.ds(pl.multiple_of(k * 16, 16), 16)

    def block(i, size=16):
        return pl.ds(pl.multiple_of(i * 16, 16), size)

    for other in others:
        remote(rhs.at[other], rhs_all.at[k], 5, {"tm": other}).start()
    count = pl.ds(0, groups - 1)
    to_owners = remote(rhs.at[count], rhs_all.at[count], 5, {"tm": after})
    rhs_all[k] = rhs[k]

    st = stacks(jnp.concatenate([halo_v1, change1], axis=0))
    rest1 = rest1 + scattered(st[0], st[1], t_change0 - sent_scale * change1)
    base0 = base0 + halves(dot(place, split(jnp.concatenate([change0, rest], axis=0))))
    first_last.wait()
    delta = sigma * timed(jnp.where(started, before0[...], 0.0))
    v1_0 = base0 + delta
    step = sigma * (rest1 + timed(delta))
    carry[...] = v0_1 + sigma * timed(v1_0 - v1_1)
    carried = remote(carry, before_carry, 6, {"tm": after})
    carried.start()
    pre0 = v1_0 - step
    pre1 = v1_1 + step
    sent_pre0 = chosen(pre0)
    sent_pre1 = chosen(pre1)
    pre1 = step

    m2 = halves(dot(split(m1), w1))
    w2 = weights(m2)
    m34 = halves(dot(split(jnp.concatenate([m1, m2], axis=0)), w2))
    m3, m4 = m34[:128], m34[128:]
    w4 = weights(m4)
    m8 = halves(dot(split(m4), w4))
    m12 = halves(dot(split(m8), w4))
    near_w[:, 256:512] = w2
    near_w[:, 512:768] = weights(m3)
    for i, w in enumerate([w4, weights(m8), weights(m12)]):
        far_w[:, i * 256 : (i + 1) * 256] = w
    own_scale = scale_full[mine, :]
    own_scale = 1.0 / (2.0 * own_scale - 1.0)
    c1 = jnp.concatenate([own_scale] * groups, axis=0)
    c2 = c1 * c1
    c4 = c2 * c2
    c8 = c4 * c4
    chain_out[0:16, :] = jnp.zeros((16, 128), F32)

    to_owners.wait()
    x = rhs_all[:, 0:16].reshape(256, 128) + later(rhs_all[:, 16:32].reshape(256, 128), 1)
    y = dot(split(x), near_w[...])
    x = (
        x
        + later(c1 * halves(y[:, 0:256]), 1)
        + later(c2 * halves(y[:, 256:512]), 2)
        + later(c1 * c2 * halves(y[:, 512:768]), 3)
    )
    y = dot(split(x), far_w[...])
    chain_out[16:272, :] = (
        x
        + later(c4 * halves(y[:, 0:256]), 4)
        + later(c8 * halves(y[:, 256:512]), 8)
        + later(c4 * c8 * halves(y[:, 512:768]), 12)
    )
    for other in others:
        remote(chain_out.at[block(other, 32)], chain_all.at[k], 7, {"tm": other}).start()
    to_slabs = remote(chain_all.at[count], chain_all.at[count], 7, {"tm": after})
    chain_all[k] = chain_out[block(k, 32), :]
    for copy in (to_slabs, carried):
        copy.wait()

    w = chain_all[:, 16:32].reshape(256, 128)
    wp = chain_all[:, 0:16].reshape(256, 128)
    c = w - v1_1
    sc = split(c)
    sp = split(wp)
    sent_c = halves(dot(choose, sc))
    sent_fc = sent_faces(sc)
    out3[0] = sent_c
    out3[1] = halves(dot(choose, sp))
    out3[2] = sent_pre0 + (1.0 + DAMPING - sent_sigma) * sent_c + sent_sigma * sent_fc
    out3[3] = sent_pre1 + KEEP * sent_c + sent_sigma * (sent_fc + timed(sent_c))
    second = [
        remote(out3.at[:, to_right], in3.at[:, to_left], 8, {"space": space(1)}),
        remote(out3.at[:, to_left], in3.at[:, to_right], 9, {"space": space(-1)}),
        remote(out3.at[0, to_right], far3.at[to_left], 10, {"space": space(2)}),
        remote(out3.at[0, to_left], far3.at[to_right], 11, {"space": space(-2)}),
    ]
    for copy in second:
        copy.start()

    fc = gather(sc, gathered)
    base0 = pre0 + (1.0 + DAMPING - sigma) * c + sigma * fc
    base1 = w + pre1 - DAMPING * c + sigma * (fc + timed(c))
    basep = before_carry[...] + KEEP * wp + sigma * (gather(sp, gathered) + timed(wp))
    basep = jnp.where(started, basep, 0.0)
    base1 = v0_1 + KEEP * base1 + sigma * (faces(base1) + timed(base0))
    base0 = v0_0 + KEEP * base0 + sigma * (faces(base0) + timed(basep))

    for copy in second:
        copy.wait()
    st = stacks(jnp.concatenate([in3[0], in3[1]] + seen_by_halo(far3[...], sent_c), axis=0))
    seen = halves(dot(halo_sent, split(st[0])))
    change = sent_sigma * seen
    change_p = sent_sigma * halves(dot(halo_sent, split(st[1])))
    extra = halo_sigma * halves(dot(far_halo, split(jnp.concatenate(st[2:4], axis=0))))
    st = stacks(jnp.concatenate([in3[2] + extra, in3[3] + extra, change], axis=0))
    t = timed(jnp.concatenate([change, change_p], axis=0))
    kept = KEEP * seen
    out_ref[1] = base1 + sigma * scattered(st[1], st[2], kept + t[0:32])
    out_ref[0] = base0 + sigma * scattered(st[0], st[2], kept + t[32:64])


def solution(mesh):
    groups, partitions = mesh.shape["tm"], mesh.shape["space"]

    def body(source, elem_scale, diag_block, block_inverse, face_flux, time_trace, neighbours, send_rows):
        any_space = pl.BlockSpec(memory_space=pl.ANY)
        vmem = pltpu.VMEM
        rows = (256, 128)
        return pl.pallas_call(
            lambda *refs: kernel(groups, partitions, *refs),
            out_shape=jax.ShapeDtypeStruct((2, 256, 128), F32),
            in_specs=[any_space] * 7,
            out_specs=pl.BlockSpec(memory_space=pltpu.VMEM),
            scratch_shapes=[
                vmem((2, 256, 128), F32), vmem((1, 256), F32), vmem((128, 128), F32), vmem((4, 128, 128), F32),
                vmem((128, 128), F32), vmem((4, 256), jnp.int32), vmem((1, 32), jnp.int32),
                vmem((1024, 256), BF16), vmem((256, 384), BF16), vmem((1024, 256), BF16),
                vmem((256, 768), BF16), vmem((256, 768), BF16), vmem((256, 1024), BF16),
                vmem(rows, F32), vmem((5, 32, 128), F32), vmem((5, 32, 128), F32), vmem((2, 32, 128), F32),
                vmem(rows, F32),
                vmem((groups, 32, 128), F32), vmem((groups, 32, 128), F32), vmem(rows, F32), vmem(rows, F32),
                vmem((16 * (groups + 1), 128), F32), vmem((groups, 32, 128), F32),
                vmem((4, 32, 128), F32), vmem((4, 32, 128), F32), vmem((32, 128), F32), vmem(rows, F32),
                pltpu.SemaphoreType.DMA((7,)), pltpu.SemaphoreType.DMA((12,)), pltpu.SemaphoreType.DMA((12,)),
            ],
            compiler_params=pltpu.CompilerParams(
                collective_id=0, has_side_effects=True, vmem_limit_bytes=32 * 1024 * 1024
            ),
        )(*[pltpu.with_memory_space_constraint(x, pltpu.HBM) for x in (source, elem_scale.reshape(1, 256), block_inverse, face_flux, time_trace, neighbours.T, send_rows)])

    return jax.shard_map(
        body,
        mesh=mesh,
        in_specs=(P("tm", "space", None), P("space"), P(), P(), P(), P(), P("space", None), P("space", None)),
        out_specs=P("tm", "space", None),
        check_vma=False,
    )
```

```python
import jax
import jax.numpy as jnp
from jax import lax
from jax.experimental import pallas as pl
from jax.experimental.pallas import tpu as pltpu
from jax.sharding import PartitionSpec as P

DAMPING = 0.7
KEEP = 1.0 - DAMPING
F32 = jnp.float32
BF16 = jnp.bfloat16
MESH = pl.DeviceIdType.MESH


def dot(left, right):
    return jnp.dot(left, right, preferred_element_type=F32)


def split(x):
    high = x.astype(BF16)
    low = (x - high.astype(F32)).astype(BF16)
    return jnp.concatenate([high, low], axis=1)


def halves(x):
    width = x.shape[1] // 2
    return x[:, :width] + x[:, width:]


def weights(matrix):
    parts = split(matrix)
    return jnp.concatenate([parts, parts], axis=0)


def iota(shape, dim):
    return lax.broadcasted_iota(jnp.int32, shape, dim)


def column(row):
    size = row.shape[1]
    same = iota((size, size), 0) == iota((size, size), 1)
    return jnp.sum(jnp.where(same, row, 0.0), axis=1, keepdims=True)


def onehot(hit):
    return jnp.where(hit, 1.0, 0.0).astype(BF16)


def any_hit(hits):
    total = jnp.where(hits[0], 1.0, 0.0)
    for hit in hits[1:]:
        total = total + jnp.where(hit, 1.0, 0.0)
    return total.astype(BF16)


def later(blocks, by):
    zeros = jnp.zeros((16 * by, blocks.shape[1]), F32)
    return jnp.concatenate([zeros, blocks[: -16 * by]], axis=0)


def kernel(
    groups, partitions,
    source_hbm, scale_hbm, inverse_hbm, flux_hbm, trace_hbm, neighbours_hbm, send_hbm,
    out_ref,
    source, scale_row, inverse, flux, trace, neighbours, send_row,
    pick, spread, face_w, near_w, far_w, gathered,
    v0_last, out1, in1, far1, before0,
    rhs, rhs_all, carry, before_carry, chain_out, chain_all, out3, in3, far3, scale_full,
    in_sem, send_sem, recv_sem,
):
    k = lax.axis_index("tm")
    p = lax.axis_index("space")
    loads = [
        pltpu.make_async_copy(src, dst, in_sem.at[i])
        for i, (src, dst) in enumerate(
            [
                (scale_hbm, scale_row), (send_hbm, send_row), (neighbours_hbm, neighbours), (inverse_hbm, inverse),
                (source_hbm, source), (flux_hbm, flux), (trace_hbm, trace),
            ]
        )
    ]
    for load in loads:
        load.start()

    def space(by):
        return lax.rem(p + partitions + by, partitions)

    others = []
    for hops in (4, 3, 2, 1):
        for dy in range(4):
            for dx in range(4):
                if min(dy, 4 - dy) + min(dx, 4 - dx) == hops:
                    others.append(lax.rem(k // 4 + dy, 4) * 4 + lax.rem(lax.rem(k, 4) + dx, 4))
    after = lax.rem(k + 1, groups)

    barrier = pltpu.get_barrier_semaphore()
    senders = [{"tm": other} for other in others]
    senders += [{"space": space(by)} for by in (1, -1, 2, -2)]
    for partner in senders:
        pl.semaphore_signal(barrier, inc=1, device_id=partner, device_id_type=MESH)

    def remote(src, dst, number, device):
        return pltpu.make_async_remote_copy(
            src_ref=src, dst_ref=dst, send_sem=send_sem.at[number], recv_sem=recv_sem.at[number],
            device_id=device, device_id_type=MESH,
        )

    for load in loads[:3]:
        load.wait()
    scale = column(scale_row[...])
    scale_full[...] = jnp.broadcast_to(scale, (256, 128))
    sigma = DAMPING / scale
    coarse = 1.0 / (2.0 * scale - 1.0)
    send_f = send_row[...].astype(F32)
    send_col = column(send_f)
    lanes = iota((256, 256), 1).astype(F32)
    choose_hit = iota((32, 256), 1).astype(F32) == send_col
    choose = onehot(choose_hit)
    sent_scale = jnp.sum(jnp.where(choose_hit, scale_row[...], 0.0), axis=1, keepdims=True)
    sent_sigma = DAMPING / sent_scale
    name_rows = [neighbours[f : f + 1, :].astype(F32) for f in range(4)]
    sent_names = [jnp.sum(jnp.where(choose_hit, row, 0.0), axis=1, keepdims=True) for row in name_rows]
    wide = iota((32, 256), 1).astype(F32)
    sent_pick = jnp.concatenate([onehot(wide == names) for names in sent_names], axis=0)

    def halo_hits(names, size):
        lane = iota((size, 128), 1)
        hits = []
        for f in range(4):
            target = jnp.where(lane // 32 == f, lane % 32 + 256, -1).astype(F32)
            hits.append(target == names[f])
        return any_hit(hits)

    halo_sent = halo_hits(sent_names, 32)
    lane = iota((32, 128), 1)
    facts = jnp.where(lane == 4, sent_sigma, 0.0)
    for f in range(4):
        facts = facts + jnp.where(lane == f, sent_names[f], 0.0)
    out1[4] = facts

    loads[3].wait()
    inverse_w = weights(inverse[...])
    loads[4].wait()
    v0_0 = sigma * halves(dot(split(source[0]), inverse_w))
    v0_1 = sigma * halves(dot(split(source[1]), inverse_w))
    v0_last[...] = v0_1
    a0 = v0_0 * scale * (1.0 / DAMPING)
    a1 = v0_1 * scale * (1.0 / DAMPING)
    for load in loads[5:]:
        load.wait()
    flux_b = halves(dot(split(flux[...].reshape(512, 128)), inverse_w))
    for f in range(4):
        face_w[f * 256 : (f + 1) * 256, :] = weights(flux_b[f * 128 : (f + 1) * 128])
    m1 = halves(dot(split(trace[...]), inverse_w))
    w1 = weights(m1)
    near_w[:, 0:256] = w1
    s0 = split(v0_0)
    s1 = split(v0_1)
    own0 = halves(dot(choose, s0))
    own1 = halves(dot(choose, s1))
    out1[0] = own0
    out1[1] = own1

    def timed(x):
        return halves(dot(split(x), near_w[:, 0:256]))

    def sent_faces(parts):
        rows = dot(sent_pick, parts).astype(BF16)
        rows = jnp.concatenate([rows[f * 32 : (f + 1) * 32] for f in range(4)], axis=1)
        return halves(dot(rows, face_w[...]))

    out1[2] = (1.0 + KEEP) * own0 + sent_sigma * sent_faces(s0)
    out1[3] = (1.0 + KEEP) * own1 + sent_sigma * (sent_faces(s1) + timed(own0))
    pl.semaphore_wait(barrier, groups + 3)

    to_right, to_left = pl.ds(16, 16), pl.ds(0, 16)
    first = [
        remote(out1.at[:, to_right], in1.at[:, to_left], 0, {"space": space(1)}),
        remote(out1.at[:, to_left], in1.at[:, to_right], 1, {"space": space(-1)}),
        remote(out1.at[0:2, to_right], far1.at[:, to_left], 2, {"space": space(2)}),
        remote(out1.at[0:2, to_left], far1.at[:, to_right], 3, {"space": space(-2)}),
    ]
    first_last = remote(v0_last, before0, 4, {"tm": after})
    for copy in first + [first_last]:
        copy.start()

    send4 = jnp.concatenate([send_col] * 4, axis=0)
    eye = iota((128, 128), 0) == iota((128, 128), 1)
    send4 = jnp.sum(jnp.where(eye, send4, 0.0), axis=0, keepdims=True)
    names = [column(row) for row in name_rows]
    for f in range(4):
        pick[f * 256 : (f + 1) * 256, :] = onehot(lanes == names[f])
    spread[:, 0:128] = halo_hits(names, 256)
    lane = iota((256, 128), 1)
    spread[:, 128:256] = any_hit([(jnp.where(lane // 32 == f, send4, -1.0) == names[f]) for f in range(4)])
    element = iota((256, 128), 0).astype(F32)
    spread[:, 256:384] = onehot(jnp.where(lane < 32, send4, -1.0) == element)

    def gather(parts, ref):
        for f in range(4):
            rows = dot(pick[f * 256 : (f + 1) * 256, :], parts)
            ref[:, f * 256 : (f + 1) * 256] = rows.astype(BF16)
        return halves(dot(ref[...], face_w[...]))

    def faces(x):
        return gather(split(x), gathered)

    def stacks(rows):
        parts = split(rows)
        each = [halves(dot(parts, face_w[f * 256 : (f + 1) * 256, :])) for f in range(4)]
        count = rows.shape[0] // 32
        return [jnp.concatenate([e[i * 32 : (i + 1) * 32] for e in each], axis=0) for i in range(count)]

    def scattered(halo_stack, change_stack, own_rows):
        rest = jnp.zeros((96, 128), F32)
        right = jnp.concatenate([halo_stack, change_stack, own_rows, rest], axis=0)
        return halves(dot(spread[...], split(right)))

    def chosen(x):
        return halves(dot(choose, split(x)))

    base1 = (1.0 + KEEP) * v0_1 + sigma * (gather(s1, gathered) + timed(v0_0))
    base0 = (1.0 + KEEP) * v0_0 + sigma * gather(s0, gathered)
    rest1 = a1 - scale * base1 + faces(base1) + timed(base0)
    rest0 = a0 - scale * base0 + faces(base0)
    onward = sigma * timed(v0_1)
    onward = faces(onward) + timed(onward) - scale * onward

    for copy in first:
        copy.wait_recv()
    started = k > 0
    facts = in1[4]
    far_names = [facts[:, f : f + 1] for f in range(4)]
    halo_sigma = facts[:, 4:5]
    far_hits = halo_hits(far_names, 32).astype(F32)
    upper = iota((32, 128), 0) < 16
    far_halo = jnp.concatenate([jnp.where(upper, far_hits, 0.0), jnp.where(upper, 0.0, far_hits)], axis=1).astype(BF16)

    def seen_by_halo(far, own):
        return [far[0:16], own[0:16], own[16:32], far[16:32]]

    st = stacks(
        jnp.concatenate([in1[0], in1[1]] + seen_by_halo(far1[0], own0) + seen_by_halo(far1[1], own1), axis=0)
    )
    change0 = sent_sigma * halves(dot(halo_sent, split(st[0])))
    change1 = sent_sigma * halves(dot(halo_sent, split(st[1])))
    halo_v0 = in1[2] + halo_sigma * halves(dot(far_halo, split(jnp.concatenate(st[2:4], axis=0))))
    halo_v1 = in1[3] + halo_sigma * halves(dot(far_halo, split(jnp.concatenate(st[4:6], axis=0))))
    change = change0 + change1
    t_change0 = timed(change0)
    st = stacks(jnp.concatenate([halo_v0 + halo_v1, change, halo_sigma * timed(in1[1])], axis=0))
    total = rest0 + rest1 + scattered(st[0], st[1], t_change0 - sent_scale * change)
    onward = onward + halves(dot(spread[:, 0:128], split(st[2])))
    place = spread[:, 256:384]
    rest = jnp.zeros((96, 128), F32)
    v1_1 = base1 + halves(dot(place, split(jnp.concatenate([change1, rest], axis=0))))
    rhs[:, 0:16] = (coarse * total + v1_1).reshape(groups, 16, 128)
    rhs[:, 16:32] = (coarse * onward).reshape(groups, 16, 128)
    mine = pl.ds(pl.multiple_of(k * 16, 16), 16)

    def block(i, size=16):
        return pl.ds(pl.multiple_of(i * 16, 16), size)

    for other in others:
        remote(rhs.at[other], rhs_all.at[k], 5, {"tm": other}).start()
    count = pl.ds(0, groups - 1)
    to_owners = remote(rhs.at[count], rhs_all.at[count], 5, {"tm": after})
    rhs_all[k] = rhs[k]

    st = stacks(jnp.concatenate([halo_v1, change1], axis=0))
    rest1 = rest1 + scattered(st[0], st[1], t_change0 - sent_scale * change1)
    base0 = base0 + halves(dot(place, split(jnp.concatenate([change0, rest], axis=0))))
    first_last.wait_recv()
    delta = sigma * timed(jnp.where(started, before0[...], 0.0))
    v1_0 = base0 + delta
    step = sigma * (rest1 + timed(delta))
    carry[...] = v0_1 + sigma * timed(v1_0 - v1_1)
    carried = remote(carry, before_carry, 6, {"tm": after})
    pre0 = v1_0 - step
    pre1 = v1_1 + step
    sent_pre0 = chosen(pre0)
    sent_pre1 = chosen(pre1)
    pre1 = step

    m2 = halves(dot(split(m1), w1))
    w2 = weights(m2)
    m34 = halves(dot(split(jnp.concatenate([m1, m2], axis=0)), w2))
    m3, m4 = m34[:128], m34[128:]
    w4 = weights(m4)
    m8 = halves(dot(split(m4), w4))
    m12 = halves(dot(split(m8), w4))
    near_w[:, 256:512] = w2
    near_w[:, 512:768] = weights(m3)
    for i, w in enumerate([w4, weights(m8), weights(m12)]):
        far_w[:, i * 256 : (i + 1) * 256] = w
    own_scale = scale_full[mine, :]
    own_scale = 1.0 / (2.0 * own_scale - 1.0)
    c1 = jnp.concatenate([own_scale] * groups, axis=0)
    c2 = c1 * c1
    c4 = c2 * c2
    c8 = c4 * c4
    chain_out[0:16, :] = jnp.zeros((16, 128), F32)

    to_owners.wait_recv()
    x = rhs_all[:, 0:16].reshape(256, 128) + later(rhs_all[:, 16:32].reshape(256, 128), 1)
    y = dot(split(x), near_w[...])
    x = (
        x
        + later(c1 * halves(y[:, 0:256]), 1)
        + later(c2 * halves(y[:, 256:512]), 2)
        + later(c1 * c2 * halves(y[:, 512:768]), 3)
    )
    y = dot(split(x), far_w[...])
    chain_out[16:272, :] = (
        x
        + later(c4 * halves(y[:, 0:256]), 4)
        + later(c8 * halves(y[:, 256:512]), 8)
        + later(c4 * c8 * halves(y[:, 512:768]), 12)
    )
    for other in others:
        remote(chain_out.at[block(other, 32)], chain_all.at[k], 7, {"tm": other}).start()
    to_slabs = remote(chain_all.at[count], chain_all.at[count], 7, {"tm": after})
    chain_all[k] = chain_out[block(k, 32), :]
    to_slabs.wait_send()
    carried.start()
    to_slabs.wait_recv()

    w = chain_all[:, 16:32].reshape(256, 128)
    wp = chain_all[:, 0:16].reshape(256, 128)
    c = w - v1_1
    sc = split(c)
    sp = split(wp)
    sent_c = halves(dot(choose, sc))
    sent_fc = sent_faces(sc)
    out3[0] = sent_c
    out3[1] = halves(dot(choose, sp))
    out3[2] = sent_pre0 + (1.0 + DAMPING - sent_sigma) * sent_c + sent_sigma * sent_fc
    out3[3] = sent_pre1 + KEEP * sent_c + sent_sigma * (sent_fc + timed(sent_c))
    second = [
        remote(out3.at[:, to_right], in3.at[:, to_left], 8, {"space": space(1)}),
        remote(out3.at[:, to_left], in3.at[:, to_right], 9, {"space": space(-1)}),
        remote(out3.at[0, to_right], far3.at[to_left], 10, {"space": space(2)}),
        remote(out3.at[0, to_left], far3.at[to_right], 11, {"space": space(-2)}),
    ]
    for copy in second:
        copy.start()

    fc = gather(sc, gathered)
    base0 = pre0 + (1.0 + DAMPING - sigma) * c + sigma * fc
    base1 = w + pre1 - DAMPING * c + sigma * (fc + timed(c))
    carried.wait_recv()
    basep = before_carry[...] + KEEP * wp + sigma * (gather(sp, gathered) + timed(wp))
    basep = jnp.where(started, basep, 0.0)
    base1 = v0_1 + KEEP * base1 + sigma * (faces(base1) + timed(base0))
    base0 = v0_0 + KEEP * base0 + sigma * (faces(base0) + timed(basep))

    for copy in second:
        copy.wait_recv()
    st = stacks(jnp.concatenate([in3[0], in3[1]] + seen_by_halo(far3[...], sent_c), axis=0))
    seen = halves(dot(halo_sent, split(st[0])))
    change = sent_sigma * seen
    change_p = sent_sigma * halves(dot(halo_sent, split(st[1])))
    extra = halo_sigma * halves(dot(far_halo, split(jnp.concatenate(st[2:4], axis=0))))
    st = stacks(jnp.concatenate([in3[2] + extra, in3[3] + extra, change], axis=0))
    t = timed(jnp.concatenate([change, change_p], axis=0))
    kept = KEEP * seen
    out_ref[1] = base1 + sigma * scattered(st[1], st[2], kept + t[0:32])
    out_ref[0] = base0 + sigma * scattered(st[0], st[2], kept + t[32:64])
    for copy in first + [first_last, to_owners, carried] + second:
        copy.wait_send()


def solution(mesh):
    groups, partitions = mesh.shape["tm"], mesh.shape["space"]

    def body(source, elem_scale, diag_block, block_inverse, face_flux, time_trace, neighbours, send_rows):
        any_space = pl.BlockSpec(memory_space=pl.ANY)
        vmem = pltpu.VMEM
        rows = (256, 128)
        return pl.pallas_call(
            lambda *refs: kernel(groups, partitions, *refs),
            out_shape=jax.ShapeDtypeStruct((2, 256, 128), F32),
            in_specs=[any_space] * 7,
            out_specs=pl.BlockSpec(memory_space=pltpu.VMEM),
            scratch_shapes=[
                vmem((2, 256, 128), F32), vmem((1, 256), F32), vmem((128, 128), F32), vmem((4, 128, 128), F32),
                vmem((128, 128), F32), vmem((4, 256), jnp.int32), vmem((1, 32), jnp.int32),
                vmem((1024, 256), BF16), vmem((256, 384), BF16), vmem((1024, 256), BF16),
                vmem((256, 768), BF16), vmem((256, 768), BF16), vmem((256, 1024), BF16),
                vmem(rows, F32), vmem((5, 32, 128), F32), vmem((5, 32, 128), F32), vmem((2, 32, 128), F32),
                vmem(rows, F32),
                vmem((groups, 32, 128), F32), vmem((groups, 32, 128), F32), vmem(rows, F32), vmem(rows, F32),
                vmem((16 * (groups + 1), 128), F32), vmem((groups, 32, 128), F32),
                vmem((4, 32, 128), F32), vmem((4, 32, 128), F32), vmem((32, 128), F32), vmem(rows, F32),
                pltpu.SemaphoreType.DMA((7,)), pltpu.SemaphoreType.DMA((12,)), pltpu.SemaphoreType.DMA((12,)),
            ],
            compiler_params=pltpu.CompilerParams(
                collective_id=0, has_side_effects=True, vmem_limit_bytes=32 * 1024 * 1024
            ),
        )(*[pltpu.with_memory_space_constraint(x, pltpu.HBM) for x in (source, elem_scale.reshape(1, 256), block_inverse, face_flux, time_trace, neighbours.T, send_rows)])

    return jax.shard_map(
        body,
        mesh=mesh,
        in_specs=(P("tm", "space", None), P("space"), P(), P(), P(), P(), P("space", None), P("space", None)),
        out_specs=P("tm", "space", None),
        check_vma=False,
    )
```

```python
import jax
import jax.numpy as jnp
from jax import lax
from jax.experimental import pallas as pl
from jax.experimental.pallas import tpu as pltpu
from jax.sharding import PartitionSpec as P

DAMPING = 0.7
KEEP = 1.0 - DAMPING
F32 = jnp.float32
BF16 = jnp.bfloat16
MESH = pl.DeviceIdType.MESH


def dot(left, right):
    return jnp.dot(left, right, preferred_element_type=F32)


def split(x):
    high = x.astype(BF16)
    low = (x - high.astype(F32)).astype(BF16)
    return jnp.concatenate([high, low], axis=1)


def halves(x):
    width = x.shape[1] // 2
    return x[:, :width] + x[:, width:]


def weights(matrix):
    parts = split(matrix)
    return jnp.concatenate([parts, parts], axis=0)


def iota(shape, dim):
    return lax.broadcasted_iota(jnp.int32, shape, dim)


def column(row):
    size = row.shape[1]
    same = iota((size, size), 0) == iota((size, size), 1)
    return jnp.sum(jnp.where(same, row, 0.0), axis=1, keepdims=True)


def onehot(hit):
    return jnp.where(hit, 1.0, 0.0).astype(BF16)


def any_hit(hits):
    total = jnp.where(hits[0], 1.0, 0.0)
    for hit in hits[1:]:
        total = total + jnp.where(hit, 1.0, 0.0)
    return total.astype(BF16)


def later(blocks, by):
    zeros = jnp.zeros((16 * by, blocks.shape[1]), F32)
    return jnp.concatenate([zeros, blocks[: -16 * by]], axis=0)


def kernel(
    groups, partitions,
    source_hbm, scale_hbm, inverse_hbm, flux_hbm, trace_hbm, neighbours_hbm, send_hbm,
    out_ref,
    source, scale_row, inverse, flux, trace, neighbours, send_row,
    pick, spread, face_w, near_w, far_w, gathered,
    v0_last, out1, in1, far1, before0,
    rhs, rhs_all, carry, before_carry, chain_out, chain_all, out3, in3, far3, scale_full,
    in_sem, send_sem, recv_sem, greet_sem,
):
    k = lax.axis_index("tm")
    p = lax.axis_index("space")
    loads = [
        pltpu.make_async_copy(src, dst, in_sem.at[i])
        for i, (src, dst) in enumerate(
            [
                (scale_hbm, scale_row), (send_hbm, send_row), (neighbours_hbm, neighbours), (inverse_hbm, inverse),
                (source_hbm, source), (flux_hbm, flux), (trace_hbm, trace),
            ]
        )
    ]
    def space(by):
        return lax.rem(p + partitions + by, partitions)

    others = []
    for hops in (4, 3, 2, 1):
        for dy in range(4):
            for dx in range(4):
                if min(dy, 4 - dy) + min(dx, 4 - dx) == hops:
                    others.append(lax.rem(k // 4 + dy, 4) * 4 + lax.rem(lax.rem(k, 4) + dx, 4))
    after = lax.rem(k + 1, groups)

    barrier = pltpu.get_barrier_semaphore()
    beside = [{"tm": k // 4 * 4 + lax.rem(lax.rem(k, 4) + by, 4)} for by in (2, 1, 3)]
    along = [{"tm": lax.rem(k + by, groups)} for by in (8, 4, 12)]
    senders = [{"tm": lax.rem(k + groups - 1, groups)}] + beside + along
    senders += [{"space": space(by)} for by in (2, -2, 1, -1)]
    for partner in senders:
        pl.semaphore_signal(barrier, inc=1, device_id=partner, device_id_type=MESH)
    for load in loads:
        load.start()

    def remote(src, dst, number, device):
        return pltpu.make_async_remote_copy(
            src_ref=src, dst_ref=dst, send_sem=send_sem.at[number], recv_sem=recv_sem.at[number],
            device_id=device, device_id_type=MESH,
        )

    for load in loads[:3]:
        load.wait()
    scale = column(scale_row[...])
    scale_full[...] = jnp.broadcast_to(scale, (256, 128))
    sigma = DAMPING / scale
    coarse = 1.0 / (2.0 * scale - 1.0)
    send_f = send_row[...].astype(F32)
    send_col = column(send_f)
    lanes = iota((256, 256), 1).astype(F32)
    choose_hit = iota((32, 256), 1).astype(F32) == send_col
    choose = onehot(choose_hit)
    sent_scale = jnp.sum(jnp.where(choose_hit, scale_row[...], 0.0), axis=1, keepdims=True)
    sent_sigma = DAMPING / sent_scale
    name_rows = [neighbours[f : f + 1, :].astype(F32) for f in range(4)]
    sent_names = [jnp.sum(jnp.where(choose_hit, row, 0.0), axis=1, keepdims=True) for row in name_rows]
    wide = iota((32, 256), 1).astype(F32)
    sent_pick = jnp.concatenate([onehot(wide == names) for names in sent_names], axis=0)

    def halo_hits(names, size):
        lane = iota((size, 128), 1)
        hits = []
        for f in range(4):
            target = jnp.where(lane // 32 == f, lane % 32 + 256, -1).astype(F32)
            hits.append(target == names[f])
        return any_hit(hits)

    halo_sent = halo_hits(sent_names, 32)
    lane = iota((32, 128), 1)
    facts = jnp.where(lane == 4, sent_sigma, 0.0)
    for f in range(4):
        facts = facts + jnp.where(lane == f, sent_names[f], 0.0)
    out1[3] = facts

    loads[3].wait()
    inverse_w = weights(inverse[...])
    loads[4].wait()
    v0_0 = sigma * halves(dot(split(source[0]), inverse_w))
    v0_1 = sigma * halves(dot(split(source[1]), inverse_w))
    v0_last[...] = v0_1
    a0 = v0_0 * scale * (1.0 / DAMPING)
    a1 = v0_1 * scale * (1.0 / DAMPING)
    for load in loads[5:]:
        load.wait()
    flux_b = halves(dot(split(flux[...].reshape(512, 128)), inverse_w))
    for f in range(4):
        face_w[f * 256 : (f + 1) * 256, :] = weights(flux_b[f * 128 : (f + 1) * 128])
    m1 = halves(dot(split(trace[...]), inverse_w))
    w1 = weights(m1)
    near_w[:, 0:256] = w1
    s0 = split(v0_0)
    s1 = split(v0_1)
    own0 = halves(dot(choose, s0))
    own1 = halves(dot(choose, s1))
    out1[0] = own0
    out1[1] = own1

    def timed(x):
        return halves(dot(split(x), near_w[:, 0:256]))

    def sent_faces(parts):
        rows = dot(sent_pick, parts).astype(BF16)
        rows = jnp.concatenate([rows[f * 32 : (f + 1) * 32] for f in range(4)], axis=1)
        return halves(dot(rows, face_w[...]))

    part1 = (1.0 + KEEP) * own1 + sent_sigma * (sent_faces(s1) + timed(own0))
    own_sum = own0 + own1
    out1[2] = part1 + (1.0 + KEEP) * own0 + sent_sigma * sent_faces(s0)
    out1[4] = part1
    out1[5] = own_sum
    pl.semaphore_wait(barrier, 11)

    to_right, to_left = pl.ds(16, 16), pl.ds(0, 16)
    first = [
        remote(out1.at[0:4, to_right], in1.at[0:4, to_left], 0, {"space": space(1)}),
        remote(out1.at[0:4, to_left], in1.at[0:4, to_right], 1, {"space": space(-1)}),
        remote(out1.at[5, to_right], far1.at[0, to_left], 2, {"space": space(2)}),
        remote(out1.at[5, to_left], far1.at[0, to_right], 3, {"space": space(-2)}),
    ]
    late = [
        remote(out1.at[4, to_right], in1.at[4, to_left], 6, {"space": space(1)}),
        remote(out1.at[4, to_left], in1.at[4, to_right], 7, {"space": space(-1)}),
        remote(out1.at[1, to_right], far1.at[1, to_left], 8, {"space": space(2)}),
        remote(out1.at[1, to_left], far1.at[1, to_right], 9, {"space": space(-2)}),
    ]
    first_last = remote(v0_last, before0, 10, {"tm": after})
    for copy in first + late + [first_last]:
        copy.start()

    for partner in along:
        pl.semaphore_signal(greet_sem, inc=1, device_id=partner, device_id_type=MESH)

    send4 = jnp.concatenate([send_col] * 4, axis=0)
    eye = iota((128, 128), 0) == iota((128, 128), 1)
    send4 = jnp.sum(jnp.where(eye, send4, 0.0), axis=0, keepdims=True)
    names = [column(row) for row in name_rows]
    for f in range(4):
        pick[f * 256 : (f + 1) * 256, :] = onehot(lanes == names[f])
    spread[:, 0:128] = halo_hits(names, 256)
    lane = iota((256, 128), 1)
    spread[:, 128:256] = any_hit([(jnp.where(lane // 32 == f, send4, -1.0) == names[f]) for f in range(4)])
    element = iota((256, 128), 0).astype(F32)
    spread[:, 256:384] = onehot(jnp.where(lane < 32, send4, -1.0) == element)

    def gather(parts, ref):
        for f in range(4):
            rows = dot(pick[f * 256 : (f + 1) * 256, :], parts)
            ref[:, f * 256 : (f + 1) * 256] = rows.astype(BF16)
        return halves(dot(ref[...], face_w[...]))

    def faces(x):
        return gather(split(x), gathered)

    def stacks(rows):
        parts = split(rows)
        each = [halves(dot(parts, face_w[f * 256 : (f + 1) * 256, :])) for f in range(4)]
        count = rows.shape[0] // 32
        return [jnp.concatenate([e[i * 32 : (i + 1) * 32] for e in each], axis=0) for i in range(count)]

    def scattered(halo_stack, change_stack, own_rows):
        rest = jnp.zeros((96, 128), F32)
        right = jnp.concatenate([halo_stack, change_stack, own_rows, rest], axis=0)
        return halves(dot(spread[...], split(right)))

    def chosen(x):
        return halves(dot(choose, split(x)))

    mine = pl.ds(pl.multiple_of(k * 16, 16), 16)

    def block(i, size=16):
        return pl.ds(pl.multiple_of(i * 16, 16), size)

    base1 = (1.0 + KEEP) * v0_1 + sigma * (gather(s1, gathered) + timed(v0_0))
    base0 = (1.0 + KEEP) * v0_0 + sigma * gather(s0, gathered)
    rest1 = a1 - scale * base1 + faces(base1) + timed(base0)
    rest0 = a0 - scale * base0 + faces(base0)
    onward = sigma * timed(v0_1)
    onward = faces(onward) + timed(onward) - scale * onward

    for copy in first:
        copy.wait_recv()
    started = k > 0
    facts = in1[3]
    far_names = [facts[:, f : f + 1] for f in range(4)]
    halo_sigma = facts[:, 4:5]
    far_hits = halo_hits(far_names, 32).astype(F32)
    upper = iota((32, 128), 0) < 16
    far_halo = jnp.concatenate([jnp.where(upper, far_hits, 0.0), jnp.where(upper, 0.0, far_hits)], axis=1).astype(BF16)

    def seen_by_halo(far, own):
        return [far[0:16], own[0:16], own[16:32], far[16:32]]

    st = stacks(jnp.concatenate([in1[0], in1[1]] + seen_by_halo(far1[0], own_sum), axis=0))
    change0 = sent_sigma * halves(dot(halo_sent, split(st[0])))
    change1 = sent_sigma * halves(dot(halo_sent, split(st[1])))
    halo_sum = in1[2] + halo_sigma * halves(dot(far_halo, split(jnp.concatenate(st[2:4], axis=0))))
    change = change0 + change1
    t_change0 = timed(change0)
    st = stacks(jnp.concatenate([halo_sum, change, halo_sigma * timed(in1[1])], axis=0))
    total = rest0 + rest1 + scattered(st[0], st[1], t_change0 - sent_scale * change)
    onward = onward + halves(dot(spread[:, 0:128], split(st[2])))
    place = spread[:, 256:384]
    rest = jnp.zeros((96, 128), F32)
    v1_1 = base1 + halves(dot(place, split(jnp.concatenate([change1, rest], axis=0))))
    rhs[:, 0:16] = (coarse * total + v1_1).reshape(groups, 16, 128)
    rhs[:, 16:32] = (coarse * onward).reshape(groups, 16, 128)
    pl.semaphore_wait(greet_sem, 3)
    for other in others:
        remote(rhs.at[other], rhs_all.at[k], 12, {"tm": other}).start()
    to_owners = remote(rhs.at[0 : groups - 1], rhs_all.at[0 : groups - 1], 12, {"tm": after})
    rhs_all[k] = rhs[k]

    for copy in late:
        copy.wait_recv()
    st = stacks(jnp.concatenate(seen_by_halo(far1[1], own1), axis=0))
    halo_v1 = in1[4] + halo_sigma * halves(dot(far_halo, split(jnp.concatenate(st, axis=0))))
    st = stacks(jnp.concatenate([halo_v1, change1], axis=0))
    rest1 = rest1 + scattered(st[0], st[1], t_change0 - sent_scale * change1)
    base0 = base0 + halves(dot(place, split(jnp.concatenate([change0, rest], axis=0))))
    first_last.wait_recv()
    delta = sigma * timed(jnp.where(started, before0[...], 0.0))
    v1_0 = base0 + delta
    step = sigma * (rest1 + timed(delta))
    carry[...] = v0_1 + sigma * timed(v1_0 - v1_1)
    carried = remote(carry, before_carry, 13, {"tm": after})
    pre0 = v1_0 - step
    pre1 = v1_1 + step
    sent_pre0 = chosen(pre0)
    sent_pre1 = chosen(pre1)
    pre1 = step

    m2 = halves(dot(split(m1), w1))
    w2 = weights(m2)
    m34 = halves(dot(split(jnp.concatenate([m1, m2], axis=0)), w2))
    m3, m4 = m34[:128], m34[128:]
    w4 = weights(m4)
    m8 = halves(dot(split(m4), w4))
    m12 = halves(dot(split(m8), w4))
    near_w[:, 256:512] = w2
    near_w[:, 512:768] = weights(m3)
    for i, w in enumerate([w4, weights(m8), weights(m12)]):
        far_w[:, i * 256 : (i + 1) * 256] = w
    own_scale = scale_full[mine, :]
    own_scale = 1.0 / (2.0 * own_scale - 1.0)
    c1 = jnp.concatenate([own_scale] * groups, axis=0)
    c2 = c1 * c1
    c4 = c2 * c2
    c8 = c4 * c4
    chain_out[0:16, :] = jnp.zeros((16, 128), F32)

    to_owners.wait_recv()
    x = rhs_all[:, 0:16].reshape(256, 128) + later(rhs_all[:, 16:32].reshape(256, 128), 1)
    y = dot(split(x), near_w[...])
    x = (
        x
        + later(c1 * halves(y[:, 0:256]), 1)
        + later(c2 * halves(y[:, 256:512]), 2)
        + later(c1 * c2 * halves(y[:, 512:768]), 3)
    )
    y = dot(split(x), far_w[...])
    chain_out[16:272, :] = (
        x
        + later(c4 * halves(y[:, 0:256]), 4)
        + later(c8 * halves(y[:, 256:512]), 8)
        + later(c4 * c8 * halves(y[:, 512:768]), 12)
    )
    for other in others:
        remote(chain_out.at[block(other, 32)], chain_all.at[k], 14, {"tm": other}).start()
    to_slabs = remote(chain_all.at[0 : groups - 1], chain_all.at[0 : groups - 1], 14, {"tm": after})
    chain_all[k] = chain_out[block(k, 32), :]
    to_slabs.wait_send()
    carried.start()
    to_slabs.wait_recv()

    w = chain_all[:, 16:32].reshape(256, 128)
    wp = chain_all[:, 0:16].reshape(256, 128)
    c = w - v1_1
    sc = split(c)
    sp = split(wp)
    sent_c = halves(dot(choose, sc))
    sent_fc = sent_faces(sc)
    out3[0] = sent_c
    out3[1] = halves(dot(choose, sp))
    out3[2] = sent_pre0 + (1.0 + DAMPING - sent_sigma) * sent_c + sent_sigma * sent_fc
    out3[3] = sent_pre1 + KEEP * sent_c + sent_sigma * (sent_fc + timed(sent_c))
    second = [
        remote(out3.at[:, to_right], in3.at[:, to_left], 15, {"space": space(1)}),
        remote(out3.at[:, to_left], in3.at[:, to_right], 16, {"space": space(-1)}),
        remote(out3.at[0, to_right], far3.at[to_left], 17, {"space": space(2)}),
        remote(out3.at[0, to_left], far3.at[to_right], 18, {"space": space(-2)}),
    ]
    for copy in second:
        copy.start()

    fc = gather(sc, gathered)
    base0 = pre0 + (1.0 + DAMPING - sigma) * c + sigma * fc
    base1 = w + pre1 - DAMPING * c + sigma * (fc + timed(c))
    carried.wait_recv()
    basep = before_carry[...] + KEEP * wp + sigma * (gather(sp, gathered) + timed(wp))
    basep = jnp.where(started, basep, 0.0)
    base1 = v0_1 + KEEP * base1 + sigma * (faces(base1) + timed(base0))
    base0 = v0_0 + KEEP * base0 + sigma * (faces(base0) + timed(basep))

    for copy in second:
        copy.wait_recv()
    st = stacks(jnp.concatenate([in3[0], in3[1]] + seen_by_halo(far3[...], sent_c), axis=0))
    seen = halves(dot(halo_sent, split(st[0])))
    change = sent_sigma * seen
    change_p = sent_sigma * halves(dot(halo_sent, split(st[1])))
    extra = halo_sigma * halves(dot(far_halo, split(jnp.concatenate(st[2:4], axis=0))))
    st = stacks(jnp.concatenate([in3[2] + extra, in3[3] + extra, change], axis=0))
    t = timed(jnp.concatenate([change, change_p], axis=0))
    kept = KEEP * seen
    out_ref[1] = base1 + sigma * scattered(st[1], st[2], kept + t[0:32])
    out_ref[0] = base0 + sigma * scattered(st[0], st[2], kept + t[32:64])
    for copy in first + late + [first_last, to_owners, carried] + second:
        copy.wait_send()


def solution(mesh):
    groups, partitions = mesh.shape["tm"], mesh.shape["space"]

    def body(source, elem_scale, diag_block, block_inverse, face_flux, time_trace, neighbours, send_rows):
        any_space = pl.BlockSpec(memory_space=pl.ANY)
        vmem = pltpu.VMEM
        rows = (256, 128)
        return pl.pallas_call(
            lambda *refs: kernel(groups, partitions, *refs),
            out_shape=jax.ShapeDtypeStruct((2, 256, 128), F32),
            in_specs=[any_space] * 7,
            out_specs=pl.BlockSpec(memory_space=pltpu.VMEM),
            scratch_shapes=[
                vmem((2, 256, 128), F32), vmem((1, 256), F32), vmem((128, 128), F32), vmem((4, 128, 128), F32),
                vmem((128, 128), F32), vmem((4, 256), jnp.int32), vmem((1, 32), jnp.int32),
                vmem((1024, 256), BF16), vmem((256, 384), BF16), vmem((1024, 256), BF16),
                vmem((256, 768), BF16), vmem((256, 768), BF16), vmem((256, 1024), BF16),
                vmem(rows, F32), vmem((6, 32, 128), F32), vmem((5, 32, 128), F32), vmem((2, 32, 128), F32),
                vmem(rows, F32),
                vmem((groups, 32, 128), F32), vmem((groups, 32, 128), F32), vmem(rows, F32), vmem(rows, F32),
                vmem((16 * (groups + 1), 128), F32), vmem((groups, 32, 128), F32),
                vmem((4, 32, 128), F32), vmem((4, 32, 128), F32), vmem((32, 128), F32), vmem(rows, F32),
                pltpu.SemaphoreType.DMA((7,)), pltpu.SemaphoreType.DMA((19,)), pltpu.SemaphoreType.DMA((19,)),
                pltpu.SemaphoreType.REGULAR,
            ],
            compiler_params=pltpu.CompilerParams(
                collective_id=0, has_side_effects=True, vmem_limit_bytes=32 * 1024 * 1024
            ),
        )(*[pltpu.with_memory_space_constraint(x, pltpu.HBM) for x in (source, elem_scale.reshape(1, 256), block_inverse, face_flux, time_trace, neighbours.T, send_rows)])

    return jax.shard_map(
        body,
        mesh=mesh,
        in_specs=(P("tm", "space", None), P("space"), P(), P(), P(), P(), P("space", None), P("space", None)),
        out_specs=P("tm", "space", None),
        check_vma=False,
    )
```

```python
import jax
import jax.numpy as jnp
from jax import lax
from jax.experimental import pallas as pl
from jax.experimental.pallas import tpu as pltpu
from jax.sharding import PartitionSpec as P

DAMPING = 0.7
KEEP = 1.0 - DAMPING
F32 = jnp.float32
BF16 = jnp.bfloat16
MESH = pl.DeviceIdType.MESH


def dot(left, right):
    return jnp.dot(left, right, preferred_element_type=F32)


def split(x):
    high = x.astype(BF16)
    low = (x - high.astype(F32)).astype(BF16)
    return jnp.concatenate([high, low], axis=1)


def halves(x):
    width = x.shape[1] // 2
    return x[:, :width] + x[:, width:]


def weights(matrix):
    parts = split(matrix)
    return jnp.concatenate([parts, parts], axis=0)


def iota(shape, dim):
    return lax.broadcasted_iota(jnp.int32, shape, dim)


def column(row):
    size = row.shape[1]
    same = iota((size, size), 0) == iota((size, size), 1)
    return jnp.sum(jnp.where(same, row, 0.0), axis=1, keepdims=True)


def onehot(hit):
    return jnp.where(hit, 1.0, 0.0).astype(BF16)


def any_hit(hits):
    total = jnp.where(hits[0], 1.0, 0.0)
    for hit in hits[1:]:
        total = total + jnp.where(hit, 1.0, 0.0)
    return total.astype(BF16)


def later(blocks, by):
    zeros = jnp.zeros((16 * by, blocks.shape[1]), F32)
    return jnp.concatenate([zeros, blocks[: -16 * by]], axis=0)


def kernel(
    groups, partitions,
    source_hbm, scale_hbm, inverse_hbm, flux_hbm, trace_hbm, neighbours_hbm, send_hbm,
    out_ref,
    source, scale_row, inverse, flux, trace, neighbours, send_row,
    pick, spread, face_w, near_w, far_w, gathered,
    v0_last, out1, in1, far1, before0,
    rhs, rhs_all, carry, before_carry, chain_out, chain_all, out3, in3, far3, scale_full,
    in_sem, send_sem, recv_sem, greet_sem,
):
    k = lax.axis_index("tm")
    p = lax.axis_index("space")
    loads = [
        pltpu.make_async_copy(src, dst, in_sem.at[i])
        for i, (src, dst) in enumerate(
            [
                (scale_hbm, scale_row), (send_hbm, send_row), (neighbours_hbm, neighbours), (inverse_hbm, inverse),
                (source_hbm, source), (flux_hbm, flux), (trace_hbm, trace),
            ]
        )
    ]
    def space(by):
        return lax.rem(p + partitions + by, partitions)

    others = []
    for hops in (4, 3, 2, 1):
        for dy in range(4):
            for dx in range(4):
                if min(dy, 4 - dy) + min(dx, 4 - dx) == hops:
                    others.append(lax.rem(k // 4 + dy, 4) * 4 + lax.rem(lax.rem(k, 4) + dx, 4))
    after = lax.rem(k + 1, groups)

    barrier = pltpu.get_barrier_semaphore()
    beside = [{"tm": k // 4 * 4 + lax.rem(lax.rem(k, 4) + by, 4)} for by in (2, 1, 3)]
    along = [{"tm": lax.rem(k + by, groups)} for by in (8, 4, 12)]
    senders = [{"tm": lax.rem(k + groups - 1, groups)}] + beside + along
    senders += [{"space": space(by)} for by in (2, -2, 1, -1)]
    for partner in senders:
        pl.semaphore_signal(barrier, inc=1, device_id=partner, device_id_type=MESH)
    for load in loads:
        load.start()

    def remote(src, dst, number, device):
        return pltpu.make_async_remote_copy(
            src_ref=src, dst_ref=dst, send_sem=send_sem.at[number], recv_sem=recv_sem.at[number],
            device_id=device, device_id_type=MESH,
        )

    for load in loads[:3]:
        load.wait()
    scale = column(scale_row[...])
    scale_full[...] = jnp.broadcast_to(scale, (256, 128))
    sigma = DAMPING / scale
    coarse = 1.0 / (2.0 * scale - 1.0)
    send_f = send_row[...].astype(F32)
    send_col = column(send_f)
    lanes = iota((256, 256), 1).astype(F32)
    choose_hit = iota((32, 256), 1).astype(F32) == send_col
    choose = onehot(choose_hit)
    sent_scale = jnp.sum(jnp.where(choose_hit, scale_row[...], 0.0), axis=1, keepdims=True)
    sent_sigma = DAMPING / sent_scale
    name_rows = [neighbours[f : f + 1, :].astype(F32) for f in range(4)]
    sent_names = [jnp.sum(jnp.where(choose_hit, row, 0.0), axis=1, keepdims=True) for row in name_rows]
    wide = iota((32, 256), 1).astype(F32)
    sent_pick = jnp.concatenate([onehot(wide == names) for names in sent_names], axis=0)

    def halo_hits(names, size):
        lane = iota((size, 128), 1)
        hits = []
        for f in range(4):
            target = jnp.where(lane // 32 == f, lane % 32 + 256, -1).astype(F32)
            hits.append(target == names[f])
        return any_hit(hits)

    halo_sent = halo_hits(sent_names, 32)
    lane = iota((32, 128), 1)
    facts = jnp.where(lane == 4, sent_sigma, 0.0)
    for f in range(4):
        facts = facts + jnp.where(lane == f, sent_names[f], 0.0)
    out1[3] = facts

    loads[3].wait()
    inverse_w = weights(inverse[...])
    loads[4].wait()
    v0_0 = sigma * halves(dot(split(source[0]), inverse_w))
    v0_1 = sigma * halves(dot(split(source[1]), inverse_w))
    v0_last[...] = v0_1
    a0 = v0_0 * scale * (1.0 / DAMPING)
    a1 = v0_1 * scale * (1.0 / DAMPING)
    for load in loads[5:]:
        load.wait()
    flux_b = halves(dot(split(flux[...].reshape(512, 128)), inverse_w))
    for f in range(4):
        face_w[f * 256 : (f + 1) * 256, :] = weights(flux_b[f * 128 : (f + 1) * 128])
    m1 = halves(dot(split(trace[...]), inverse_w))
    w1 = weights(m1)
    near_w[:, 0:256] = w1
    s0 = split(v0_0)
    s1 = split(v0_1)
    own0 = halves(dot(choose, s0))
    own1 = halves(dot(choose, s1))
    out1[0] = own0
    out1[1] = own1

    def timed(x):
        return halves(dot(split(x), near_w[:, 0:256]))

    def named(rows):
        rows = rows.astype(BF16)
        rows = jnp.concatenate([rows[f * 32 : (f + 1) * 32] for f in range(4)], axis=1)
        return halves(dot(rows, face_w[...]))

    def sent_faces(parts):
        return named(dot(sent_pick, parts))

    part1 = (1.0 + KEEP) * own1 + sent_sigma * (sent_faces(s1) + timed(own0))
    own_sum = own0 + own1
    out1[2] = part1 + (1.0 + KEEP) * own0 + sent_sigma * sent_faces(s0)
    out1[4] = part1
    out1[5] = own_sum
    pl.semaphore_wait(barrier, 11)

    to_right, to_left = pl.ds(16, 16), pl.ds(0, 16)
    first = [
        remote(out1.at[0:4, to_right], in1.at[0:4, to_left], 0, {"space": space(1)}),
        remote(out1.at[0:4, to_left], in1.at[0:4, to_right], 1, {"space": space(-1)}),
        remote(out1.at[5, to_right], far1.at[0, to_left], 2, {"space": space(2)}),
        remote(out1.at[5, to_left], far1.at[0, to_right], 3, {"space": space(-2)}),
    ]
    late = [
        remote(out1.at[4, to_right], in1.at[4, to_left], 6, {"space": space(1)}),
        remote(out1.at[4, to_left], in1.at[4, to_right], 7, {"space": space(-1)}),
        remote(out1.at[1, to_right], far1.at[1, to_left], 8, {"space": space(2)}),
        remote(out1.at[1, to_left], far1.at[1, to_right], 9, {"space": space(-2)}),
    ]
    first_last = remote(v0_last, before0, 10, {"tm": after})
    for copy in first + late + [first_last]:
        copy.start()

    for partner in along:
        pl.semaphore_signal(greet_sem, inc=1, device_id=partner, device_id_type=MESH)

    send4 = jnp.concatenate([send_col] * 4, axis=0)
    eye = iota((128, 128), 0) == iota((128, 128), 1)
    send4 = jnp.sum(jnp.where(eye, send4, 0.0), axis=0, keepdims=True)
    names = [column(row) for row in name_rows]
    for f in range(4):
        pick[f * 256 : (f + 1) * 256, :] = onehot(lanes == names[f])
    spread[:, 0:128] = halo_hits(names, 256)
    lane = iota((256, 128), 1)
    spread[:, 128:256] = any_hit([(jnp.where(lane // 32 == f, send4, -1.0) == names[f]) for f in range(4)])
    element = iota((256, 128), 0).astype(F32)
    spread[:, 256:384] = onehot(jnp.where(lane < 32, send4, -1.0) == element)

    def gather(parts, slot):
        for f in range(4):
            rows = dot(pick[f * 256 : (f + 1) * 256, :], parts)
            gathered[slot, :, f * 256 : (f + 1) * 256] = rows.astype(BF16)
        return halves(dot(gathered[slot], face_w[...]))

    def faces(x, slot):
        return gather(split(x), slot)

    def stacks(rows):
        parts = split(rows)
        each = [halves(dot(parts, face_w[f * 256 : (f + 1) * 256, :])) for f in range(4)]
        count = rows.shape[0] // 32
        return [jnp.concatenate([e[i * 32 : (i + 1) * 32] for e in each], axis=0) for i in range(count)]

    def scattered(halo_stack, change_stack, own_rows):
        rest = jnp.zeros((96, 128), F32)
        right = jnp.concatenate([halo_stack, change_stack, own_rows, rest], axis=0)
        return halves(dot(spread[...], split(right)))

    def chosen(x):
        return halves(dot(choose, split(x)))

    mine = pl.ds(pl.multiple_of(k * 16, 16), 16)

    def block(i, size=16):
        return pl.ds(pl.multiple_of(i * 16, 16), size)

    base1 = (1.0 + KEEP) * v0_1 + sigma * (gather(s1, 0) + timed(v0_0))
    base0 = (1.0 + KEEP) * v0_0 + sigma * gather(s0, 1)
    rest1 = a1 - scale * base1 + faces(base1, 2) + timed(base0)
    rest0 = a0 - scale * base0 + faces(base0, 3)
    onward = sigma * timed(v0_1)
    onward = coarse * (faces(onward, 4) + timed(onward) - scale * onward)
    ready = coarse * (rest0 + rest1) + base1

    for copy in first:
        copy.wait_recv()
    started = k > 0
    facts = in1[3]
    far_names = [facts[:, f : f + 1] for f in range(4)]
    halo_sigma = facts[:, 4:5]
    far_hits = halo_hits(far_names, 32).astype(F32)
    upper = iota((32, 128), 0) < 16
    far_halo = jnp.concatenate([jnp.where(upper, far_hits, 0.0), jnp.where(upper, 0.0, far_hits)], axis=1).astype(BF16)

    def seen_by_halo(far, own):
        return [far[0:16], own[0:16], own[16:32], far[16:32]]

    st = stacks(jnp.concatenate([in1[0], in1[1]] + seen_by_halo(far1[0], own_sum), axis=0))
    change0 = sent_sigma * halves(dot(halo_sent, split(st[0])))
    change1 = sent_sigma * halves(dot(halo_sent, split(st[1])))
    halo_sum = in1[2] + halo_sigma * halves(dot(far_halo, split(jnp.concatenate(st[2:4], axis=0))))
    change = change0 + change1
    t_change0 = timed(change0)
    st = stacks(jnp.concatenate([halo_sum, change, halo_sigma * timed(in1[1])], axis=0))
    own_rows = t_change0 - sent_scale * change + (2.0 * sent_scale - 1.0) * change1
    rhs[:, 0:16] = (ready + coarse * scattered(st[0], st[1], own_rows)).reshape(groups, 16, 128)
    onward = onward + coarse * halves(dot(spread[:, 0:128], split(st[2])))
    rhs[:, 16:32] = onward.reshape(groups, 16, 128)
    pl.semaphore_wait(greet_sem, 3)
    for other in others:
        remote(rhs.at[other], rhs_all.at[k], 12, {"tm": other}).start()
    to_owners = remote(rhs.at[0 : groups - 1], rhs_all.at[0 : groups - 1], 12, {"tm": after})
    rhs_all[k] = rhs[k]

    for copy in late:
        copy.wait_recv()
    st = stacks(jnp.concatenate(seen_by_halo(far1[1], own1), axis=0))
    halo_v1 = in1[4] + halo_sigma * halves(dot(far_halo, split(jnp.concatenate(st, axis=0))))
    place = spread[:, 256:384]
    rest = jnp.zeros((96, 128), F32)
    v1_1 = base1 + halves(dot(place, split(jnp.concatenate([change1, rest], axis=0))))
    st = stacks(jnp.concatenate([halo_v1, change1], axis=0))
    rest1 = rest1 + scattered(st[0], st[1], t_change0 - sent_scale * change1)
    base0 = base0 + halves(dot(place, split(jnp.concatenate([change0, rest], axis=0))))
    first_last.wait_recv()
    delta = sigma * timed(jnp.where(started, before0[...], 0.0))
    v1_0 = base0 + delta
    step = sigma * (rest1 + timed(delta))
    carry[...] = v0_1 + sigma * timed(v1_0 - v1_1)
    carried = remote(carry, before_carry, 13, {"tm": after})
    pre0 = v1_0 - step
    pre1 = v1_1 + step
    sent_pre0 = chosen(pre0)
    sent_pre1 = chosen(pre1)
    pre1 = step

    m2 = halves(dot(split(m1), w1))
    w2 = weights(m2)
    m34 = halves(dot(split(jnp.concatenate([m1, m2], axis=0)), w2))
    m3, m4 = m34[:128], m34[128:]
    w4 = weights(m4)
    m8 = halves(dot(split(m4), w4))
    m12 = halves(dot(split(m8), w4))
    near_w[:, 256:512] = w2
    near_w[:, 512:768] = weights(m3)
    for i, w in enumerate([w4, weights(m8), weights(m12)]):
        far_w[:, i * 256 : (i + 1) * 256] = w
    own_scale = scale_full[mine, :]
    own_scale = 1.0 / (2.0 * own_scale - 1.0)
    c1 = jnp.concatenate([own_scale] * groups, axis=0)
    c2 = c1 * c1
    c4 = c2 * c2
    c8 = c4 * c4
    chain_out[0:16, :] = jnp.zeros((16, 128), F32)

    to_owners.wait_recv()
    x = rhs_all[:, 0:16].reshape(256, 128) + later(rhs_all[:, 16:32].reshape(256, 128), 1)
    y = dot(split(x), near_w[...])
    x = (
        x
        + later(c1 * halves(y[:, 0:256]), 1)
        + later(c2 * halves(y[:, 256:512]), 2)
        + later(c1 * c2 * halves(y[:, 512:768]), 3)
    )
    y = dot(split(x), far_w[...])
    chain_out[16:272, :] = (
        x
        + later(c4 * halves(y[:, 0:256]), 4)
        + later(c8 * halves(y[:, 256:512]), 8)
        + later(c4 * c8 * halves(y[:, 512:768]), 12)
    )
    for other in others:
        remote(chain_out.at[block(other, 32)], chain_all.at[k], 14, {"tm": other}).start()
    to_slabs = remote(chain_all.at[0 : groups - 1], chain_all.at[0 : groups - 1], 14, {"tm": after})
    chain_all[k] = chain_out[block(k, 32), :]
    to_slabs.wait_send()
    carried.start()
    to_slabs.wait_recv()

    w = chain_all[:, 16:32].reshape(256, 128)
    wp = chain_all[:, 0:16].reshape(256, 128)
    c = w - v1_1
    sc = split(c)
    sp = split(wp)
    rows = dot(jnp.concatenate([sent_pick, choose], axis=0), sc)
    sent_c = halves(rows[128:160])
    sent_fc = named(rows[0:128])
    out3[0] = sent_c
    out3[1] = halves(dot(choose, sp))
    out3[2] = sent_pre0 + (1.0 + DAMPING - sent_sigma) * sent_c + sent_sigma * sent_fc
    out3[3] = sent_pre1 + KEEP * sent_c + sent_sigma * (sent_fc + timed(sent_c))
    second = [
        remote(out3.at[:, to_right], in3.at[:, to_left], 15, {"space": space(1)}),
        remote(out3.at[:, to_left], in3.at[:, to_right], 16, {"space": space(-1)}),
        remote(out3.at[0, to_right], far3.at[to_left], 17, {"space": space(2)}),
        remote(out3.at[0, to_left], far3.at[to_right], 18, {"space": space(-2)}),
    ]
    for copy in second:
        copy.start()

    fc = gather(sc, 5)
    base0 = pre0 + (1.0 + DAMPING - sigma) * c + sigma * fc
    base1 = w + pre1 - DAMPING * c + sigma * (fc + timed(c))
    carried.wait_recv()
    basep = before_carry[...] + KEEP * wp + sigma * (gather(sp, 6) + timed(wp))
    basep = jnp.where(started, basep, 0.0)
    base1 = v0_1 + KEEP * base1 + sigma * (faces(base1, 7) + timed(base0))
    base0 = v0_0 + KEEP * base0 + sigma * (faces(base0, 8) + timed(basep))

    for copy in second:
        copy.wait_recv()
    st = stacks(jnp.concatenate([in3[0], in3[1]] + seen_by_halo(far3[...], sent_c), axis=0))
    seen = halves(dot(halo_sent, split(st[0])))
    change = sent_sigma * seen
    change_p = sent_sigma * halves(dot(halo_sent, split(st[1])))
    extra = halo_sigma * halves(dot(far_halo, split(jnp.concatenate(st[2:4], axis=0))))
    st = stacks(jnp.concatenate([in3[2] + extra, in3[3] + extra, change], axis=0))
    t = timed(jnp.concatenate([change, change_p], axis=0))
    kept = KEEP * seen
    out_ref[1] = base1 + sigma * scattered(st[1], st[2], kept + t[0:32])
    out_ref[0] = base0 + sigma * scattered(st[0], st[2], kept + t[32:64])
    for copy in first + late + [first_last, to_owners, carried] + second:
        copy.wait_send()


def solution(mesh):
    groups, partitions = mesh.shape["tm"], mesh.shape["space"]

    def body(source, elem_scale, diag_block, block_inverse, face_flux, time_trace, neighbours, send_rows):
        any_space = pl.BlockSpec(memory_space=pl.ANY)
        vmem = pltpu.VMEM
        rows = (256, 128)
        return pl.pallas_call(
            lambda *refs: kernel(groups, partitions, *refs),
            out_shape=jax.ShapeDtypeStruct((2, 256, 128), F32),
            in_specs=[any_space] * 7,
            out_specs=pl.BlockSpec(memory_space=pltpu.VMEM),
            scratch_shapes=[
                vmem((2, 256, 128), F32), vmem((1, 256), F32), vmem((128, 128), F32), vmem((4, 128, 128), F32),
                vmem((128, 128), F32), vmem((4, 256), jnp.int32), vmem((1, 32), jnp.int32),
                vmem((1024, 256), BF16), vmem((256, 384), BF16), vmem((1024, 256), BF16),
                vmem((256, 768), BF16), vmem((256, 768), BF16), vmem((9, 256, 1024), BF16),
                vmem(rows, F32), vmem((6, 32, 128), F32), vmem((5, 32, 128), F32), vmem((2, 32, 128), F32),
                vmem(rows, F32),
                vmem((groups, 32, 128), F32), vmem((groups, 32, 128), F32), vmem(rows, F32), vmem(rows, F32),
                vmem((16 * (groups + 1), 128), F32), vmem((groups, 32, 128), F32),
                vmem((4, 32, 128), F32), vmem((4, 32, 128), F32), vmem((32, 128), F32), vmem(rows, F32),
                pltpu.SemaphoreType.DMA((7,)), pltpu.SemaphoreType.DMA((19,)), pltpu.SemaphoreType.DMA((19,)),
                pltpu.SemaphoreType.REGULAR,
            ],
            compiler_params=pltpu.CompilerParams(
                collective_id=0, has_side_effects=True, vmem_limit_bytes=32 * 1024 * 1024
            ),
        )(*[pltpu.with_memory_space_constraint(x, pltpu.HBM) for x in (source, elem_scale.reshape(1, 256), block_inverse, face_flux, time_trace, neighbours.T, send_rows)])

    return jax.shard_map(
        body,
        mesh=mesh,
        in_specs=(P("tm", "space", None), P("space"), P(), P(), P(), P(), P("space", None), P("space", None)),
        out_specs=P("tm", "space", None),
        check_vma=False,
    )
```

```python
import jax
import jax.numpy as jnp
from jax import lax
from jax.experimental import pallas as pl
from jax.experimental.pallas import tpu as pltpu
from jax.sharding import PartitionSpec as P

DAMPING = 0.7
KEEP = 1.0 - DAMPING
F32 = jnp.float32
BF16 = jnp.bfloat16
MESH = pl.DeviceIdType.MESH


def dot(left, right):
    return jnp.dot(left, right, preferred_element_type=F32)


def split(x):
    high = x.astype(BF16)
    low = (x - high.astype(F32)).astype(BF16)
    return jnp.concatenate([high, low], axis=1)


def halves(x):
    width = x.shape[1] // 2
    return x[:, :width] + x[:, width:]


def weights(matrix):
    parts = split(matrix)
    return jnp.concatenate([parts, parts], axis=0)


def iota(shape, dim):
    return lax.broadcasted_iota(jnp.int32, shape, dim)


def column(row):
    size = row.shape[1]
    same = iota((size, size), 0) == iota((size, size), 1)
    return jnp.sum(jnp.where(same, row, 0.0), axis=1, keepdims=True)


def onehot(hit):
    return jnp.where(hit, 1.0, 0.0).astype(BF16)


def any_hit(hits):
    total = jnp.where(hits[0], 1.0, 0.0)
    for hit in hits[1:]:
        total = total + jnp.where(hit, 1.0, 0.0)
    return total.astype(BF16)


def later(blocks, by):
    zeros = jnp.zeros((16 * by, blocks.shape[1]), F32)
    return jnp.concatenate([zeros, blocks[: -16 * by]], axis=0)


def kernel(
    groups, partitions,
    source_hbm, scale_hbm, inverse_hbm, flux_hbm, trace_hbm, neighbours_hbm, send_hbm,
    out_ref,
    source, scale_row, inverse, flux, trace, neighbours, send_row,
    pick, spread, face_w, near_w, far_w, gathered,
    v0_last, out1, in1, far1, before0,
    rhs, rhs_all, carry, before_carry, chain_out, chain_all, out3, in3, far3, scale_full,
    in_sem, send_sem, recv_sem, greet_sem,
):
    k = lax.axis_index("tm")
    p = lax.axis_index("space")
    loads = [
        pltpu.make_async_copy(src, dst, in_sem.at[i])
        for i, (src, dst) in enumerate(
            [
                (scale_hbm, scale_row), (send_hbm, send_row), (neighbours_hbm, neighbours), (inverse_hbm, inverse),
                (source_hbm, source), (flux_hbm, flux), (trace_hbm, trace),
            ]
        )
    ]
    def space(by):
        return lax.rem(p + partitions + by, partitions)

    others = []
    for hops in (4, 3, 2, 1):
        for dy in range(4):
            for dx in range(4):
                if min(dy, 4 - dy) + min(dx, 4 - dx) == hops:
                    others.append(lax.rem(k // 4 + dy, 4) * 4 + lax.rem(lax.rem(k, 4) + dx, 4))
    after = lax.rem(k + 1, groups)

    barrier = pltpu.get_barrier_semaphore()
    beside = [{"tm": k // 4 * 4 + lax.rem(lax.rem(k, 4) + by, 4)} for by in (2, 1, 3)]
    along = [{"tm": lax.rem(k + by, groups)} for by in (8, 4, 12)]
    senders = [{"tm": lax.rem(k + groups - 1, groups)}] + beside + along
    senders += [{"space": space(by)} for by in (2, -2, 1, -1)]
    for partner in senders:
        pl.semaphore_signal(barrier, inc=1, device_id=partner, device_id_type=MESH)
    for load in loads:
        load.start()

    def remote(src, dst, number, device):
        return pltpu.make_async_remote_copy(
            src_ref=src, dst_ref=dst, send_sem=send_sem.at[number], recv_sem=recv_sem.at[number],
            device_id=device, device_id_type=MESH,
        )

    for load in loads[:3]:
        load.wait()
    scale = column(scale_row[...])
    scale_full[...] = jnp.broadcast_to(scale, (256, 128))
    sigma = DAMPING / scale
    coarse = 1.0 / (2.0 * scale - 1.0)
    send_f = send_row[...].astype(F32)
    send_col = column(send_f)
    lanes = iota((256, 256), 1).astype(F32)
    choose_hit = iota((32, 256), 1).astype(F32) == send_col
    choose = onehot(choose_hit)
    sent_scale = jnp.sum(jnp.where(choose_hit, scale_row[...], 0.0), axis=1, keepdims=True)
    sent_sigma = DAMPING / sent_scale
    name_rows = [neighbours[f : f + 1, :].astype(F32) for f in range(4)]
    sent_names = [jnp.sum(jnp.where(choose_hit, row, 0.0), axis=1, keepdims=True) for row in name_rows]
    wide = iota((32, 256), 1).astype(F32)
    sent_pick = jnp.concatenate([onehot(wide == names) for names in sent_names], axis=0)

    def halo_hits(names, size):
        lane = iota((size, 128), 1)
        hits = []
        for f in range(4):
            target = jnp.where(lane // 32 == f, lane % 32 + 256, -1).astype(F32)
            hits.append(target == names[f])
        return any_hit(hits)

    halo_sent = halo_hits(sent_names, 32)
    lane = iota((32, 128), 1)
    facts = jnp.where(lane == 4, sent_sigma, 0.0)
    for f in range(4):
        facts = facts + jnp.where(lane == f, sent_names[f], 0.0)
    out1[3] = facts

    loads[3].wait()
    inverse_w = weights(inverse[...])
    loads[4].wait()
    v0_0 = sigma * halves(dot(split(source[0]), inverse_w))
    v0_1 = sigma * halves(dot(split(source[1]), inverse_w))
    v0_last[...] = v0_1
    a0 = v0_0 * scale * (1.0 / DAMPING)
    a1 = v0_1 * scale * (1.0 / DAMPING)
    for load in loads[5:]:
        load.wait()
    flux_b = halves(dot(split(flux[...].reshape(512, 128)), inverse_w))
    for f in range(4):
        face_w[f * 256 : (f + 1) * 256, :] = weights(flux_b[f * 128 : (f + 1) * 128])
    m1 = halves(dot(split(trace[...]), inverse_w))
    w1 = weights(m1)
    near_w[:, 0:256] = w1
    s0 = split(v0_0)
    s1 = split(v0_1)
    own0 = halves(dot(choose, s0))
    own1 = halves(dot(choose, s1))
    out1[0] = own0
    out1[1] = own1

    def timed(x):
        return halves(dot(split(x), near_w[:, 0:256]))

    def named(rows):
        rows = rows.astype(BF16)
        rows = jnp.concatenate([rows[f * 32 : (f + 1) * 32] for f in range(4)], axis=1)
        return halves(dot(rows, face_w[...]))

    def sent_faces(parts):
        return named(dot(sent_pick, parts))

    part1 = (1.0 + KEEP) * own1 + sent_sigma * (sent_faces(s1) + timed(own0))
    own_sum = own0 + own1
    out1[2] = part1 + (1.0 + KEEP) * own0 + sent_sigma * sent_faces(s0)
    out1[4] = part1
    out1[5] = own_sum
    pl.semaphore_wait(barrier, 11)

    to_right, to_left = pl.ds(16, 16), pl.ds(0, 16)
    first = [
        remote(out1.at[0:4, to_right], in1.at[0:4, to_left], 0, {"space": space(1)}),
        remote(out1.at[0:4, to_left], in1.at[0:4, to_right], 1, {"space": space(-1)}),
        remote(out1.at[5, to_right], far1.at[0, to_left], 2, {"space": space(2)}),
        remote(out1.at[5, to_left], far1.at[0, to_right], 3, {"space": space(-2)}),
    ]
    late = [
        remote(out1.at[4, to_right], in1.at[4, to_left], 6, {"space": space(1)}),
        remote(out1.at[4, to_left], in1.at[4, to_right], 7, {"space": space(-1)}),
        remote(out1.at[1, to_right], far1.at[1, to_left], 8, {"space": space(2)}),
        remote(out1.at[1, to_left], far1.at[1, to_right], 9, {"space": space(-2)}),
    ]
    first_last = remote(v0_last, before0, 10, {"tm": after})
    for copy in first + [first_last]:
        copy.start()

    for partner in along:
        pl.semaphore_signal(greet_sem, inc=1, device_id=partner, device_id_type=MESH)

    send4 = jnp.concatenate([send_col] * 4, axis=0)
    eye = iota((128, 128), 0) == iota((128, 128), 1)
    send4 = jnp.sum(jnp.where(eye, send4, 0.0), axis=0, keepdims=True)
    names = [column(row) for row in name_rows]
    for f in range(4):
        pick[f * 256 : (f + 1) * 256, :] = onehot(lanes == names[f])
    spread[:, 0:128] = halo_hits(names, 256)
    lane = iota((256, 128), 1)
    spread[:, 128:256] = any_hit([(jnp.where(lane // 32 == f, send4, -1.0) == names[f]) for f in range(4)])
    element = iota((256, 128), 0).astype(F32)
    spread[:, 256:384] = onehot(jnp.where(lane < 32, send4, -1.0) == element)

    def gather(parts, slot):
        for f in range(4):
            rows = dot(pick[f * 256 : (f + 1) * 256, :], parts)
            gathered[slot, :, f * 256 : (f + 1) * 256] = rows.astype(BF16)
        return halves(dot(gathered[slot], face_w[...]))

    def faces(x, slot):
        return gather(split(x), slot)

    def stacks(rows):
        parts = split(rows)
        each = [halves(dot(parts, face_w[f * 256 : (f + 1) * 256, :])) for f in range(4)]
        count = rows.shape[0] // 32
        return [jnp.concatenate([e[i * 32 : (i + 1) * 32] for e in each], axis=0) for i in range(count)]

    def scattered(halo_stack, change_stack, own_rows):
        rest = jnp.zeros((96, 128), F32)
        right = jnp.concatenate([halo_stack, change_stack, own_rows, rest], axis=0)
        return halves(dot(spread[...], split(right)))

    def chosen(x):
        return halves(dot(choose, split(x)))

    mine = pl.ds(pl.multiple_of(k * 16, 16), 16)

    def block(i, size=16):
        return pl.ds(pl.multiple_of(i * 16, 16), size)

    base1 = (1.0 + KEEP) * v0_1 + sigma * (gather(s1, 0) + timed(v0_0))
    base0 = (1.0 + KEEP) * v0_0 + sigma * gather(s0, 1)
    rest1 = a1 - scale * base1 + faces(base1, 2) + timed(base0)
    rest0 = a0 - scale * base0 + faces(base0, 3)
    onward = sigma * timed(v0_1)
    onward = coarse * (faces(onward, 4) + timed(onward) - scale * onward)
    ready = coarse * (rest0 + rest1) + base1

    for copy in late:
        copy.start()
    for copy in first:
        copy.wait_recv()
    started = k > 0
    facts = in1[3]
    far_names = [facts[:, f : f + 1] for f in range(4)]
    halo_sigma = facts[:, 4:5]
    far_hits = halo_hits(far_names, 32).astype(F32)
    upper = iota((32, 128), 0) < 16
    far_halo = jnp.concatenate([jnp.where(upper, far_hits, 0.0), jnp.where(upper, 0.0, far_hits)], axis=1).astype(BF16)

    def seen_by_halo(far, own):
        return [far[0:16], own[0:16], own[16:32], far[16:32]]

    st = stacks(jnp.concatenate([in1[0], in1[1]] + seen_by_halo(far1[0], own_sum), axis=0))
    change0 = sent_sigma * halves(dot(halo_sent, split(st[0])))
    change1 = sent_sigma * halves(dot(halo_sent, split(st[1])))
    halo_sum = in1[2] + halo_sigma * halves(dot(far_halo, split(jnp.concatenate(st[2:4], axis=0))))
    change = change0 + change1
    t_change0 = timed(change0)
    st = stacks(jnp.concatenate([halo_sum, change, halo_sigma * timed(in1[1])], axis=0))
    own_rows = t_change0 - sent_scale * change + (2.0 * sent_scale - 1.0) * change1
    rhs[:, 0:16] = (ready + coarse * scattered(st[0], st[1], own_rows)).reshape(groups, 16, 128)
    onward = onward + coarse * halves(dot(spread[:, 0:128], split(st[2])))
    rhs[:, 16:32] = onward.reshape(groups, 16, 128)
    pl.semaphore_wait(greet_sem, 3)
    for other in others:
        remote(rhs.at[other], rhs_all.at[k], 12, {"tm": other}).start()
    to_owners = remote(rhs.at[0 : groups - 1], rhs_all.at[0 : groups - 1], 12, {"tm": after})
    rhs_all[k] = rhs[k]

    for copy in late:
        copy.wait_recv()
    st = stacks(jnp.concatenate(seen_by_halo(far1[1], own1), axis=0))
    halo_v1 = in1[4] + halo_sigma * halves(dot(far_halo, split(jnp.concatenate(st, axis=0))))
    place = spread[:, 256:384]
    rest = jnp.zeros((96, 128), F32)
    v1_1 = base1 + halves(dot(place, split(jnp.concatenate([change1, rest], axis=0))))
    st = stacks(jnp.concatenate([halo_v1, change1], axis=0))
    rest1 = rest1 + scattered(st[0], st[1], t_change0 - sent_scale * change1)
    base0 = base0 + halves(dot(place, split(jnp.concatenate([change0, rest], axis=0))))
    first_last.wait_recv()
    delta = sigma * timed(jnp.where(started, before0[...], 0.0))
    v1_0 = base0 + delta
    step = sigma * (rest1 + timed(delta))
    carry[...] = v0_1 + sigma * timed(v1_0 - v1_1)
    carried = remote(carry, before_carry, 13, {"tm": after})
    pre0 = v1_0 - step
    pre1 = v1_1 + step
    sent_pre0 = chosen(pre0)
    sent_pre1 = chosen(pre1)
    pre1 = step

    m2 = halves(dot(split(m1), w1))
    w2 = weights(m2)
    m34 = halves(dot(split(jnp.concatenate([m1, m2], axis=0)), w2))
    m3, m4 = m34[:128], m34[128:]
    w4 = weights(m4)
    m8 = halves(dot(split(m4), w4))
    m12 = halves(dot(split(m8), w4))
    near_w[:, 256:512] = w2
    near_w[:, 512:768] = weights(m3)
    for i, w in enumerate([w4, weights(m8), weights(m12)]):
        far_w[:, i * 256 : (i + 1) * 256] = w
    own_scale = scale_full[mine, :]
    own_scale = 1.0 / (2.0 * own_scale - 1.0)
    c1 = jnp.concatenate([own_scale] * groups, axis=0)
    c2 = c1 * c1
    c4 = c2 * c2
    c8 = c4 * c4
    chain_out[0:16, :] = jnp.zeros((16, 128), F32)

    to_owners.wait_recv()
    x = rhs_all[:, 0:16].reshape(256, 128) + later(rhs_all[:, 16:32].reshape(256, 128), 1)
    y = dot(split(x), near_w[...])
    x = (
        x
        + later(c1 * halves(y[:, 0:256]), 1)
        + later(c2 * halves(y[:, 256:512]), 2)
        + later(c1 * c2 * halves(y[:, 512:768]), 3)
    )
    y = dot(split(x), far_w[...])
    chain_out[16:272, :] = (
        x
        + later(c4 * halves(y[:, 0:256]), 4)
        + later(c8 * halves(y[:, 256:512]), 8)
        + later(c4 * c8 * halves(y[:, 512:768]), 12)
    )
    for other in others:
        remote(chain_out.at[block(other, 32)], chain_all.at[k], 14, {"tm": other}).start()
    to_slabs = remote(chain_all.at[0 : groups - 1], chain_all.at[0 : groups - 1], 14, {"tm": after})
    chain_all[k] = chain_out[block(k, 32), :]
    to_slabs.wait_send()
    carried.start()
    to_slabs.wait_recv()

    w = chain_all[:, 16:32].reshape(256, 128)
    wp = chain_all[:, 0:16].reshape(256, 128)
    c = w - v1_1
    sc = split(c)
    sp = split(wp)
    rows = dot(jnp.concatenate([sent_pick, choose], axis=0), sc)
    sent_c = halves(rows[128:160])
    sent_fc = named(rows[0:128])
    out3[0] = sent_c
    out3[1] = halves(dot(choose, sp))
    out3[2] = sent_pre0 + (1.0 + DAMPING - sent_sigma) * sent_c + sent_sigma * sent_fc
    out3[3] = sent_pre1 + KEEP * sent_c + sent_sigma * (sent_fc + timed(sent_c))
    second = [
        remote(out3.at[:, to_right], in3.at[:, to_left], 15, {"space": space(1)}),
        remote(out3.at[:, to_left], in3.at[:, to_right], 16, {"space": space(-1)}),
        remote(out3.at[0, to_right], far3.at[to_left], 17, {"space": space(2)}),
        remote(out3.at[0, to_left], far3.at[to_right], 18, {"space": space(-2)}),
    ]
    for copy in second:
        copy.start()

    fc = gather(sc, 5)
    base0 = pre0 + (1.0 + DAMPING - sigma) * c + sigma * fc
    base1 = w + pre1 - DAMPING * c + sigma * (fc + timed(c))
    carried.wait_recv()
    basep = before_carry[...] + KEEP * wp + sigma * (gather(sp, 6) + timed(wp))
    basep = jnp.where(started, basep, 0.0)
    base1 = v0_1 + KEEP * base1 + sigma * (faces(base1, 7) + timed(base0))
    base0 = v0_0 + KEEP * base0 + sigma * (faces(base0, 8) + timed(basep))

    for copy in second:
        copy.wait_recv()
    st = stacks(jnp.concatenate([in3[0], in3[1]] + seen_by_halo(far3[...], sent_c), axis=0))
    seen = halves(dot(halo_sent, split(st[0])))
    change = sent_sigma * seen
    change_p = sent_sigma * halves(dot(halo_sent, split(st[1])))
    extra = halo_sigma * halves(dot(far_halo, split(jnp.concatenate(st[2:4], axis=0))))
    st = stacks(jnp.concatenate([in3[2] + extra, in3[3] + extra, change], axis=0))
    t = timed(jnp.concatenate([change, change_p], axis=0))
    kept = KEEP * seen
    out_ref[1] = base1 + sigma * scattered(st[1], st[2], kept + t[0:32])
    out_ref[0] = base0 + sigma * scattered(st[0], st[2], kept + t[32:64])
    for copy in first + late + [first_last, to_owners, carried] + second:
        copy.wait_send()


def solution(mesh):
    groups, partitions = mesh.shape["tm"], mesh.shape["space"]

    def body(source, elem_scale, diag_block, block_inverse, face_flux, time_trace, neighbours, send_rows):
        any_space = pl.BlockSpec(memory_space=pl.ANY)
        vmem = pltpu.VMEM
        rows = (256, 128)
        return pl.pallas_call(
            lambda *refs: kernel(groups, partitions, *refs),
            out_shape=jax.ShapeDtypeStruct((2, 256, 128), F32),
            in_specs=[any_space] * 7,
            out_specs=pl.BlockSpec(memory_space=pltpu.VMEM),
            scratch_shapes=[
                vmem((2, 256, 128), F32), vmem((1, 256), F32), vmem((128, 128), F32), vmem((4, 128, 128), F32),
                vmem((128, 128), F32), vmem((4, 256), jnp.int32), vmem((1, 32), jnp.int32),
                vmem((1024, 256), BF16), vmem((256, 384), BF16), vmem((1024, 256), BF16),
                vmem((256, 768), BF16), vmem((256, 768), BF16), vmem((9, 256, 1024), BF16),
                vmem(rows, F32), vmem((6, 32, 128), F32), vmem((5, 32, 128), F32), vmem((2, 32, 128), F32),
                vmem(rows, F32),
                vmem((groups, 32, 128), F32), vmem((groups, 32, 128), F32), vmem(rows, F32), vmem(rows, F32),
                vmem((16 * (groups + 1), 128), F32), vmem((groups, 32, 128), F32),
                vmem((4, 32, 128), F32), vmem((4, 32, 128), F32), vmem((32, 128), F32), vmem(rows, F32),
                pltpu.SemaphoreType.DMA((7,)), pltpu.SemaphoreType.DMA((19,)), pltpu.SemaphoreType.DMA((19,)),
                pltpu.SemaphoreType.REGULAR,
            ],
            compiler_params=pltpu.CompilerParams(
                collective_id=0, has_side_effects=True, vmem_limit_bytes=32 * 1024 * 1024
            ),
        )(*[pltpu.with_memory_space_constraint(x, pltpu.HBM) for x in (source, elem_scale.reshape(1, 256), block_inverse, face_flux, time_trace, neighbours.T, send_rows)])

    return jax.shard_map(
        body,
        mesh=mesh,
        in_specs=(P("tm", "space", None), P("space"), P(), P(), P(), P(), P("space", None), P("space", None)),
        out_specs=P("tm", "space", None),
        check_vma=False,
    )
```
